128 devices in a mesh: role: 2 (over core), shard: 64 (over x, z, y).
Axes of the slice: x: 4, y: 4, z: 4, core: 2. Of those that a mesh axis runs over, the one named last changes fastest.
Arguments:
- feature_ids: int32 [2, 8, 4, 32768], P('role', None, None, 'shard'), may hold values from 0 to 3071
- labels: float32 [32768], P('shard'), may hold values from 0 to 1
- cold_rows: bfloat16 [2, 131072, 128], P('role', 'shard'), may hold values from -3 to 3
- hot_rows: bfloat16 [1024, 128], replicated, may hold values from -3 to 3
- block_owner: int32 [64, 64], P('shard'), may hold values from 0 to 63, as said below
- pushed: int32 [16384], P('shard'), may hold values from 0 to 1, as said below
- weight_in: bfloat16 [1024, 1024], replicated, may hold values from -0.1875 to 0.1875
- bias_in: bfloat16 [1024], replicated, may hold values from -3 to 3
- weight_out: bfloat16 [1024], replicated, may hold values from -0.1875 to 0.1875
Outputs:
- scores: float32 [2, 32768], P('role', 'shard')
- cold_after: bfloat16 [2, 131072, 128], P('role', 'shard')
- hot_after: bfloat16 [1024, 128], P('shard')
- weight_after: bfloat16 [1024, 1024], P('shard')
The draws below stay inside these ranges and needn't reach their ends.
Inputs may be any that keep to these rules, and one draw needn't show every extreme that they name: `feature_ids`: an id below 1024 names that hot row; an id v of 1024 or more names row v - 1024 of the device's own share of cold rows (trainer share on role 0, serving share on role 1). `block_owner`: each row and each column holds every serving device once. `pushed`: in every draw some trainer has all 4 blocks of some group marked.
All inputs are finite; a program needn't handle non-finite values.
Results may differ from the reference program's by a relative error of at most 0.01.
Values may be sent and summed in bfloat16 or wider, within the bound.
A program may use at most 128 MiB of HBM per device.

```python
import math
import jax
import jax.numpy as jnp
import numpy as np
from jax import lax

E = 128
F = 8
K = 4
H = 1024
ROW_DEV = 512
BLK = 8
CAP = 4
D_IN = 1024
ROWS_ALL = 32768
HOT = 1024
COLD_DEV = 2048
COLD_ALL = 131072
TABLE = 3072
N_SHARD = 64


def draw_block_owner(key, part):
    key = jax.random.fold_in(key, 7)
    first_key, second_key, third_key = jax.random.split(key, 3)
    owner_order = jax.random.permutation(first_key, N_SHARD)
    start_order = jax.random.permutation(second_key, N_SHARD)
    offset_order = jax.random.permutation(third_key, N_SHARD)
    return owner_order[(start_order[:, None] + offset_order[None, :]) % N_SHARD].astype(jnp.int32)


def draw_pushed(key, part):
    key = jax.random.fold_in(key, 11)
    level_key, roll_key, device_key, group_key = jax.random.split(key, 4)
    level = jax.random.randint(level_key, (N_SHARD, 1), 3, 9)
    rolled = jax.random.randint(roll_key, (N_SHARD, CAP * N_SHARD), 0, 8)
    marks = (rolled < level).astype(jnp.int32)
    device_pick = jax.random.randint(device_key, (), 0, N_SHARD)
    group_pick = jax.random.randint(group_key, (), 0, N_SHARD)
    row_pos = lax.broadcasted_iota(jnp.int32, marks.shape, 0)
    col_pos = lax.broadcasted_iota(jnp.int32, marks.shape, 1)
    filled = (row_pos == device_pick) & (col_pos // CAP == group_pick)
    return jnp.where(filled, 1, marks).reshape(-1).astype(jnp.int32)


def plant(entries, own_key, smallest, top_value):
    longest = entries.shape.index(max(entries.shape))
    spots = []
    for shift in (0, 1):
        where = [jax.random.randint(jax.random.fold_in(own_key, axis), (), 0, length) for axis, length in enumerate(entries.shape)]
        where[longest] = (where[longest] + shift) % entries.shape[longest]
        spots.append(tuple(where))
    return entries.at[spots[0]].set(smallest).at[spots[1]].set(top_value)


def steps_of(key, dims, shards, least, top_value):
    loudness = 1.0
    for axis_at, shards_of in shards:
        steps = jax.random.uniform(jax.random.fold_in(jax.random.fold_in(key, 6), axis_at), (shards_of,), jnp.float32, least / len(shards), top_value / len(shards))
        loudness = loudness * jnp.repeat(jnp.exp(steps), dims[axis_at] // shards_of).reshape((-1,) + (1,) * (len(dims) - 1 - axis_at))
    return loudness


def rank_table(count, lean):
    portions = [(1 << 20) // math.isqrt(rank ** lean) + 1 for rank in range(1, count + 1)]
    width = 1 + sum(portions) // (1 << 30)
    return np.cumsum(np.array([max(1, weight // width) for weight in portions]))


def ranked_ids(stream_key, dims, number_of, lean):
    grid = rank_table(number_of, lean)
    pick = jax.random.randint(jax.random.fold_in(stream_key, 1), dims, 0, int(grid[number_of - 1]))
    standing = jnp.searchsorted(jnp.asarray(grid, jnp.int32), pick, side="right")
    return jax.random.permutation(jax.random.fold_in(stream_key, 2), number_of)[standing].astype(jnp.int32)


def scatter_about(own_key, dims, scale, reach, cuts=(), kind=jnp.bfloat16):
    values = jax.random.normal(own_key, dims, jnp.float32) * scale
    if len(cuts) > 0:
        values = steps_of(own_key, dims, cuts, -0.22, 0.18) * values
    return jnp.clip(values, min=-reach, max=reach).astype(kind)


def setup_inputs(seed: int = 0) -> dict:
    keys = jax.random.split(jax.random.key(seed), 10)
    return {
        "feature_ids": plant(ranked_ids(keys[0], (2, F, K, ROWS_ALL), HOT + COLD_DEV, 2), jax.random.fold_in(keys[0], 3), 0, (HOT + COLD_DEV) - 1).astype(jnp.int32),
        "labels": jnp.clip(1.0 * jax.random.uniform(keys[1], (ROWS_ALL,), jnp.float32) ** steps_of(keys[1], (ROWS_ALL,), ((0, 64),), -0.2, 0.2), 0.0, 1.0),
        "cold_rows": scatter_about(keys[2], (2, COLD_ALL, E), 0.5, 3.0, ((0, 2), (1, 64))),
        "hot_rows": scatter_about(keys[3], (HOT, E), 0.5, 3.0),
        "block_owner": draw_block_owner(jax.random.fold_in(keys[9], 71), 0),
        "pushed": draw_pushed(jax.random.fold_in(keys[9], 71), 0),
        "weight_in": scatter_about(keys[6], (D_IN, H), D_IN ** -0.5, 0.1875),
        "bias_in": scatter_about(keys[7], (H,), 0.5, 3.0),
        "weight_out": scatter_about(keys[8], (H,), H ** -0.5, 0.1875),
    }


row_rate = 0.25
epsilon = 1e-06

def silu_slope(pre_act):
    gate_sig = jax.nn.sigmoid(pre_act)
    return gate_sig * (1.0 + pre_act * (1.0 - gate_sig))

def normed(grad_sum):
    return grad_sum / jnp.sqrt(jnp.mean(grad_sum * grad_sum) + epsilon)

def step_rows(old_rows, grad_rows):
    scale_rows = jnp.sqrt(lax.optimization_barrier(jnp.mean(grad_rows * grad_rows, axis=-1, keepdims=True)) + epsilon)
    return (old_rows.astype(jnp.float32) - row_rate * grad_rows / scale_rows).astype(jnp.bfloat16)

def pool_device(operands):
    ids_dev, lookup_table = operands
    running = jnp.zeros((F, ROW_DEV, E), jnp.float32)
    for bag_pos in range(K):
        running = running + lookup_table[ids_dev[:, bag_pos, :]].astype(jnp.float32)
    return jnp.transpose(running, (1, 0, 2)).reshape(ROW_DEV, F * E).astype(jnp.bfloat16)

def pool_all(ids_role, hot_table, cold_role):
    ids_dev = jnp.transpose(ids_role.reshape(F, K, N_SHARD, ROW_DEV), (2, 0, 1, 3))
    tables = jnp.concatenate([jnp.broadcast_to(hot_table[None], (N_SHARD, HOT, E)), cold_role.reshape(N_SHARD, COLD_DEV, E)], axis=1)
    return (lax.map(pool_device, (ids_dev, tables)).reshape(ROWS_ALL, D_IN), ids_dev)

def grad_device(operands):
    ids_dev, grad_dev = operands
    per_slot = jnp.transpose(grad_dev.reshape(ROW_DEV, F, E), (1, 0, 2)).astype(jnp.float32)
    values = jnp.broadcast_to(per_slot[:, None], (F, K, ROW_DEV, E)).reshape(F * K * ROW_DEV, E)
    return jax.ops.segment_sum(values, ids_dev.reshape(-1), num_segments=TABLE)

def reference(feature_ids, labels, cold_rows, hot_rows, block_owner, pushed, weight_in, bias_in, weight_out):
    pooled, ids_dev = pool_all(feature_ids[0], hot_rows, cold_rows[0])
    pre_act = jnp.dot(pooled, weight_in, preferred_element_type=jnp.float32) + bias_in.astype(jnp.float32)
    hidden = jax.nn.silu(pre_act).astype(jnp.bfloat16)
    logit = jnp.dot(hidden, weight_out, preferred_element_type=jnp.float32)
    slope_out = (jax.nn.sigmoid(logit) - labels).astype(jnp.bfloat16)
    grad_out = jnp.dot(slope_out, hidden, preferred_element_type=jnp.float32)
    grad_pre = (slope_out.astype(jnp.float32)[:, None] * weight_out.astype(jnp.float32)[None, :] * silu_slope(pre_act)).astype(jnp.bfloat16)
    grad_bias = lax.optimization_barrier(jnp.sum(grad_pre.astype(jnp.float32), axis=0))
    grad_in = jnp.dot(pooled.T, grad_pre, preferred_element_type=jnp.float32)
    grad_pooled = jnp.dot(grad_pre, weight_in.T, preferred_element_type=jnp.float32).astype(jnp.bfloat16)
    grad_tables = lax.map(grad_device, (ids_dev, grad_pooled.reshape(N_SHARD, ROW_DEV, D_IN)))
    grad_hot = lax.optimization_barrier(jnp.sum(grad_tables[:, :HOT], axis=0))
    grad_cold = grad_tables[:, HOT:].reshape(COLD_ALL, E)
    cold_learned = step_rows(cold_rows[0], grad_cold)
    hot_after = step_rows(hot_rows, grad_hot)
    weight_after = (weight_in.astype(jnp.float32) - normed(grad_in) / math.sqrt(D_IN)).astype(jnp.bfloat16)
    bias_after = (bias_in.astype(jnp.float32) - 0.5 * normed(grad_bias)).astype(jnp.bfloat16)
    out_after = (weight_out.astype(jnp.float32) - normed(grad_out) / math.sqrt(H)).astype(jnp.bfloat16)
    owner_ids = jnp.arange(N_SHARD, dtype=jnp.int32)
    owner_match = (block_owner[:, :, None] == owner_ids[None, None, :]).astype(jnp.int32)
    source_group = lax.optimization_barrier(jnp.sum(owner_match * owner_ids[None, :, None], axis=1)).astype(jnp.int32)
    learned_groups = cold_learned.reshape(N_SHARD, N_SHARD, CAP, BLK * E)
    flag_groups = pushed.reshape(N_SHARD, N_SHARD, CAP)
    sources = owner_ids[:, None]
    incoming = jnp.transpose(learned_groups[sources, source_group], (1, 0, 2, 3))
    incoming_flags = jnp.transpose(flag_groups[sources, source_group], (1, 0, 2))
    stale = cold_rows[1].reshape(N_SHARD, N_SHARD, CAP, BLK * E)
    synced = jnp.where(incoming_flags[..., None] == 1, incoming, stale).reshape(COLD_ALL, E)
    served, unused_ids = pool_all(feature_ids[1], hot_after, synced)
    pre_serve = jnp.dot(served, weight_after, preferred_element_type=jnp.float32) + bias_after.astype(jnp.float32)
    hidden_serve = jax.nn.silu(pre_serve).astype(jnp.bfloat16)
    scores_serve = jnp.dot(hidden_serve, out_after, preferred_element_type=jnp.float32)
    return (jnp.stack([logit, scores_serve]), jnp.stack([cold_learned, synced]), hot_after, weight_after)
```

```python
import math

import jax
import jax.numpy as jnp
from jax import lax
from jax.experimental import pallas as pl
from jax.experimental.pallas import tpu as pltpu
from jax.sharding import PartitionSpec as P

row_rate = 0.25
epsilon = 1e-06
unsent = 1e30
MESH = pl.DeviceIdType.MESH


def silu_slope(pre_act):
    gate_sig = jax.nn.sigmoid(pre_act)
    return gate_sig * (1.0 + pre_act * (1.0 - gate_sig))


def normed(grad_sum):
    return grad_sum / jnp.sqrt(jnp.mean(grad_sum * grad_sum) + epsilon)


def step_rows(old_rows, grad_rows):
    scale_rows = jnp.sqrt(jnp.mean(grad_rows * grad_rows, axis=-1, keepdims=True) + epsilon)
    return (old_rows.astype(jnp.float32) - row_rate * grad_rows / scale_rows).astype(jnp.bfloat16)


def pool_onehot(ids_dev, lookup_table):
    slot_count, bag_count, row_count = ids_dev.shape
    columns = lax.broadcasted_iota(jnp.int32, (row_count, lookup_table.shape[0]), 1)
    count_list = []
    pieces = []
    for slot_pos in range(slot_count):
        counts = jnp.zeros((row_count, lookup_table.shape[0]), jnp.float32)
        for bag_pos in range(bag_count):
            counts = counts + (ids_dev[slot_pos, bag_pos][:, None] == columns).astype(jnp.float32)
        counts = counts.astype(jnp.bfloat16)
        count_list.append(counts)
        pieces.append(jnp.dot(counts, lookup_table, preferred_element_type=jnp.float32))
    return (count_list, jnp.concatenate(pieces, axis=1).astype(jnp.bfloat16))


def train_step(operands):
    ids_dev, labels, lookup_table, weight_in, bias_in, weight_out = operands
    count_list, pooled = pool_onehot(ids_dev, lookup_table)
    pre_act = jnp.dot(pooled, weight_in, preferred_element_type=jnp.float32) + bias_in.astype(
        jnp.float32
    )
    hidden = jax.nn.silu(pre_act).astype(jnp.bfloat16)
    logit = jnp.dot(hidden, weight_out, preferred_element_type=jnp.float32)
    slope_out = (jax.nn.sigmoid(logit) - labels).astype(jnp.bfloat16)
    grad_out = jnp.dot(slope_out, hidden, preferred_element_type=jnp.float32)
    grad_pre = (
        slope_out.astype(jnp.float32)[:, None]
        * weight_out.astype(jnp.float32)[None, :]
        * silu_slope(pre_act)
    ).astype(jnp.bfloat16)
    grad_bias = jnp.sum(grad_pre.astype(jnp.float32), axis=0)
    grad_in = lax.dot_general(
        pooled, grad_pre, (((0,), (0,)), ((), ())), preferred_element_type=jnp.float32
    )
    grad_pooled = lax.dot_general(
        grad_pre, weight_in, (((1,), (1,)), ((), ())), preferred_element_type=jnp.float32
    ).astype(jnp.bfloat16)
    row_width = lookup_table.shape[1]
    grad_table = jnp.zeros(lookup_table.shape, jnp.float32)
    for slot_pos, counts in enumerate(count_list):
        slot_grad = grad_pooled[:, slot_pos * row_width : (slot_pos + 1) * row_width]
        grad_table = grad_table + lax.dot_general(
            counts, slot_grad, (((0,), (0,)), ((), ())), preferred_element_type=jnp.float32
        )
    return (grad_in, grad_bias, grad_out, grad_table, logit)


def spare_step(operands):
    ids_dev, labels, lookup_table, weight_in, bias_in, weight_out = operands
    return (
        jnp.zeros(weight_in.shape, jnp.float32),
        jnp.zeros(bias_in.shape, jnp.float32),
        jnp.zeros(weight_out.shape, jnp.float32),
        jnp.zeros(lookup_table.shape, jnp.float32),
        jnp.zeros(labels.shape, jnp.float32),
    )


def exchange_kernel(
    message, outgoing, hot_own, gathered, arrived, small_sum, received, piece, sends, recvs
):
    role = lax.axis_index("role")
    me = lax.axis_index("shard")
    count = message.shape[0]
    width = piece.shape[1] - 128
    barrier = pltpu.get_barrier_semaphore()

    @pl.when(role == 1)
    def _():
        def greet(step, carry):
            pl.semaphore_signal(barrier, inc=1, device_id=(0, step), device_id_type=MESH)

            @pl.when(step != me)
            def _():
                pl.semaphore_signal(barrier, inc=1, device_id=(1, step), device_id_type=MESH)

            return carry

        lax.fori_loop(0, count, greet, 0)

    @pl.when(role == 0)
    def _():
        pl.semaphore_wait(barrier, count)

        def send(step, carry):
            to = lax.rem(me + step, count)
            pltpu.make_async_remote_copy(
                message.at[to], received.at[me], sends.at[0], recvs.at[0], (1, to), MESH
            ).start()
            pltpu.make_async_remote_copy(
                outgoing.at[to], arrived.at[me], sends.at[1], recvs.at[1], (1, to), MESH
            ).start()
            return carry

        lax.fori_loop(0, count, send, 0)
        pltpu.make_async_copy(message, message, sends.at[0]).wait()
        pltpu.make_async_copy(outgoing, outgoing, sends.at[1]).wait()

    @pl.when(role == 1)
    def _():
        pltpu.make_async_copy(received, received, recvs.at[0]).wait()
        total = lax.fori_loop(
            0,
            count,
            lambda step, total: total + received[step].astype(jnp.float32),
            jnp.zeros(received.shape[1:], jnp.float32),
        )
        small_sum[...] = total[:, width + 128 :]
        piece[:, :width] = total[:, :width].astype(jnp.bfloat16)
        piece[:, width:] = step_rows(hot_own[...], total[:, width : width + 128])
        pl.semaphore_wait(barrier, count - 1)

        def send(step, carry):
            to = lax.rem(me + step, count)
            pltpu.make_async_remote_copy(
                piece, gathered.at[me], sends.at[0], recvs.at[2], (1, to), MESH
            ).start()
            return carry

        lax.fori_loop(1, count, send, 0)
        gathered[me] = piece[...]
        others = gathered.at[pl.ds(0, count - 1)]
        pltpu.make_async_copy(others, others, sends.at[0]).wait()
        pltpu.make_async_copy(others, others, recvs.at[2]).wait()
        pltpu.make_async_copy(arrived, arrived, recvs.at[1]).wait()


def exchange(message, outgoing, hot_own):
    count, rows, width = message.shape
    vmem = pl.BlockSpec(memory_space=pltpu.VMEM)
    return pl.pallas_call(
        exchange_kernel,
        out_shape=(
            jax.ShapeDtypeStruct((count, rows, width - 128), jnp.bfloat16),
            jax.ShapeDtypeStruct(outgoing.shape, jnp.bfloat16),
            jax.ShapeDtypeStruct((rows, 128), jnp.float32),
        ),
        in_specs=[vmem] * 3,
        out_specs=(vmem, vmem, vmem),
        scratch_shapes=[
            pltpu.VMEM(message.shape, jnp.bfloat16),
            pltpu.VMEM((rows, width - 128), jnp.bfloat16),
            pltpu.SemaphoreType.DMA((2,)),
            pltpu.SemaphoreType.DMA((3,)),
        ],
        compiler_params=pltpu.CompilerParams(
            collective_id=0, has_side_effects=True, vmem_limit_bytes=40 << 20
        ),
        name="exchange",
    )(message, outgoing, hot_own)


def serve_step(operands):
    ids_dev, lookup_table, weight_next, bias_next, out_next, logit = operands
    count_list, pooled = pool_onehot(ids_dev, lookup_table)
    pre_act = jnp.dot(pooled, weight_next, preferred_element_type=jnp.float32) + bias_next.astype(
        jnp.float32
    )
    hidden = jax.nn.silu(pre_act).astype(jnp.bfloat16)
    return jnp.dot(hidden, out_next, preferred_element_type=jnp.float32)


def keep_step(operands):
    return operands[5]


def on_device(
    feature_ids, labels, cold_rows, hot_rows, block_owner, pushed, weight_in, bias_in, weight_out
):
    role_index = lax.axis_index("role")
    shard_index = lax.axis_index("shard")
    shard_count = lax.axis_size("shard")
    own_ids = feature_ids[0]
    own_cold = cold_rows[0]
    hot_count = hot_rows.shape[0]
    lookup_table = jnp.concatenate([hot_rows, own_cold], axis=0)
    grad_in, grad_bias, grad_out, grad_table, logit = lax.cond(
        role_index == 0,
        train_step,
        spare_step,
        (own_ids, labels, lookup_table, weight_in, bias_in, weight_out),
    )
    cold_learned = step_rows(own_cold, grad_table[hot_count:])
    group_count = block_owner.shape[1]
    group_blocks = pushed.shape[0] // group_count
    hot_per = hot_count // shard_count
    rows_per = weight_in.shape[0] // shard_count
    small = jnp.concatenate([grad_bias, grad_out]).reshape(16, -1).astype(jnp.bfloat16)
    message = jnp.concatenate(
        [
            grad_in.astype(jnp.bfloat16).reshape(shard_count, rows_per, -1),
            grad_table[:hot_count].astype(jnp.bfloat16).reshape(shard_count, hot_per, -1),
            jnp.broadcast_to(small[None], (shard_count,) + small.shape),
        ],
        axis=2,
    )
    grouped = cold_learned.reshape(group_count, group_blocks, -1)
    grouped = jnp.where(
        pushed.reshape(group_count, group_blocks)[:, :, None] == 1, grouped, jnp.bfloat16(unsent)
    )
    owner_ids = lax.broadcasted_iota(jnp.int32, (group_count, group_count), 1)
    group_ids = lax.broadcasted_iota(jnp.int32, (group_count, group_count), 0)
    owner_match = (block_owner[0][:, None] == owner_ids).astype(jnp.int32)
    source_group = jnp.sum(owner_match * group_ids, axis=0)
    outgoing = jnp.take(grouped, source_group, axis=0).reshape(group_count, -1, own_cold.shape[1])
    hot_own = lax.dynamic_slice_in_dim(hot_rows, shard_index * hot_per, hot_per, 0)
    gathered, arrived, small_sum = exchange(message, outgoing, hot_own)
    sum_in = gathered[:, :, : weight_in.shape[1]].reshape(weight_in.shape).astype(jnp.float32)
    hot_next = gathered[:, :, weight_in.shape[1] :].reshape(hot_rows.shape)
    weight_next = (
        weight_in.astype(jnp.float32) - normed(sum_in) / math.sqrt(weight_in.shape[0])
    ).astype(jnp.bfloat16)
    sum_bias, sum_out = small_sum.reshape(2, -1)
    bias_next = (bias_in.astype(jnp.float32) - 0.5 * normed(sum_bias)).astype(jnp.bfloat16)
    out_next = (
        weight_out.astype(jnp.float32) - normed(sum_out) / math.sqrt(weight_out.shape[0])
    ).astype(jnp.bfloat16)
    arrived = arrived.reshape(own_cold.shape)
    synced = jnp.where(arrived < unsent, arrived, own_cold)
    cold_out = jnp.where(role_index == 0, cold_learned, synced)[None]
    serve_table = jnp.concatenate([hot_next, synced], axis=0)
    scores = lax.cond(
        role_index == 1,
        serve_step,
        keep_step,
        (own_ids, serve_table, weight_next, bias_next, out_next, logit),
    )
    hot_after = lax.dynamic_slice_in_dim(hot_next, shard_index * hot_per, hot_per, 0)
    weight_after = lax.dynamic_slice_in_dim(weight_next, shard_index * rows_per, rows_per, 0)
    hot_other, weight_other = lax.ppermute((hot_after, weight_after), "role", [(1, 0)])
    hot_after = jnp.where(role_index == 0, hot_other, hot_after)
    weight_after = jnp.where(role_index == 0, weight_other, weight_after)
    return (scores[None], cold_out, hot_after, weight_after)


def solution(mesh):
    in_specs = (
        P("role", None, None, "shard"),
        P("shard"),
        P("role", "shard", None),
        P(),
        P("shard", None),
        P("shard"),
        P(),
        P(),
        P(),
    )
    out_specs = (P("role", "shard"), P("role", "shard", None), P("shard", None), P("shard", None))
    return jax.shard_map(
        on_device, mesh=mesh, in_specs=in_specs, out_specs=out_specs, check_vma=False
    )
```

```python
import math

import jax
import jax.numpy as jnp
from jax import lax
from jax.experimental import pallas as pl
from jax.experimental.pallas import tpu as pltpu
from jax.sharding import PartitionSpec as P

row_rate = 0.25
epsilon = 1e-06
unsent = 1e30
BF = jnp.bfloat16
F32 = jnp.float32
MESH = pl.DeviceIdType.MESH
NN = (((1,), (0,)), ((), ()))
NT = (((1,), (1,)), ((), ()))
TN = (((0,), (0,)), ((), ()))

SHARDS = 64
SLOTS = 8
BAGS = 4
N = 512
E = 128
H = 1024
HOT = 1024
COLD = 2048
TABLE = HOT + COLD
PIECE = H // SHARDS
BLK = 8
SPAN = 256


def dot(lhs, rhs, dims=NN):
    return lax.dot_general(lhs, rhs, dims, preferred_element_type=F32)


def sigmoid(value):
    return 0.5 * jnp.tanh(0.5 * value) + 0.5


def step_rows(old_rows, grad_rows):
    scale_rows = jnp.sqrt(jnp.mean(grad_rows * grad_rows, axis=-1, keepdims=True) + epsilon)
    return old_rows.astype(F32) - row_rate * grad_rows / scale_rows


def part(index, size):
    return pl.ds(pl.multiple_of(index * size, size), size)


def identity():
    rows = lax.broadcasted_iota(jnp.int32, (E, E), 0)
    return (rows == lax.broadcasted_iota(jnp.int32, (E, E), 1)).astype(F32).astype(BF)


def first_row(value):
    return lax.broadcasted_iota(jnp.int32, (16, N), 0) == 0


def slot_rows(ids, slot):
    own = [ids[slot, bag][None, :] for bag in range(BAGS)]
    mult = [sum((one == other).astype(F32) for other in own).astype(BF) for one in own]
    return own, mult


def count_block(own, mult, block):
    spots = lax.broadcasted_iota(jnp.int32, (SPAN, N), 0).astype(F32).astype(BF)
    acc = jnp.zeros((SPAN, N), BF)
    for bag in range(BAGS):
        at = jnp.clip(own[bag] - block * SPAN, -1, SPAN).astype(F32).astype(BF)
        acc = jnp.where(spots == at, mult[bag], acc)
    return acc


def round_kernel(
    ids, labels, hot, cold, weight, bias, wout, source, pushed,
    scores, cold_out, hot_after, weight_after,
    counts, table_t, pooled_t, pre_t, hidden_t, grad_t, grad_rows, pool_acc,
    gw, rw, allw, gh, rh, allh, piece_w, piece_h, learned, outgoing, arrived, small, wide,
    next_w, sends, recvs,
):
    role = lax.axis_index("role")
    me = lax.axis_index("shard")
    barrier = pltpu.get_barrier_semaphore()

    def send_all(lo, source_of, target, sem_out, sem_in):
        def body(step, carry):
            to = lax.rem(me + step, SHARDS)
            pltpu.make_async_remote_copy(
                source_of(to), target, sem_out, sem_in, (1, to), MESH
            ).start()
            return carry

        lax.fori_loop(lo, SHARDS, body, 0)

    def drain(ref, sem):
        pltpu.make_async_copy(ref, ref, sem).wait()

    @pl.when(role == 1)
    def _():
        def greet(step, carry):
            pl.semaphore_signal(barrier, inc=1, device_id=(0, step), device_id_type=MESH)

            @pl.when(step != me)
            def _():
                pl.semaphore_signal(barrier, inc=1, device_id=(1, step), device_id_type=MESH)

            return carry

        lax.fori_loop(0, SHARDS, greet, 0)

    @pl.when(role == 0)
    def _():
        pl.semaphore_signal(barrier, inc=1, device_id=(1, me), device_id_type=MESH)
        eye = identity()
        table_t[:, :HOT] = dot(eye, hot[...], NT).astype(BF)
        table_t[:, HOT:] = dot(eye, cold[...], NT).astype(BF)

        def pool_slot(slot, carry):
            own, mult = slot_rows(ids, slot)
            lanes = part(slot, N)

            def build(block, carry):
                counts[part(block, SPAN), lanes] = count_block(own, mult, block)
                return carry

            lax.fori_loop(0, TABLE // SPAN, build, 0)
            pooled_t[part(slot, E), :] = dot(table_t[...], counts[:, lanes]).astype(BF)
            return carry

        lax.fori_loop(0, SLOTS, pool_slot, 0)
        first = lax.broadcasted_iota(jnp.int32, (16, N), 0) == 0
        ones = first.astype(F32).astype(BF)

        def forward(chunk, logit):
            cols = part(chunk, 256)
            pre = dot(weight[:, cols], pooled_t[...], TN) + dot(bias[:, cols], ones, TN)
            pre_t[cols, :] = pre
            hidden = (pre * sigmoid(pre)).astype(BF)
            hidden_t[cols, :] = hidden
            return logit + dot(wout[:, cols], hidden)

        logit = lax.fori_loop(0, H // 256, forward, jnp.zeros((16, N), F32))
        scores[...] = logit[0:1]
        slope = jnp.where(first, sigmoid(logit) - labels[...], 0.0).astype(BF)

        def backward(chunk, carry):
            cols = part(chunk, 256)
            pre = pre_t[cols, :]
            gate = sigmoid(pre)
            grad = (dot(wout[:, cols], slope, TN) * (gate * (1.0 + pre * (1.0 - gate)))).astype(BF)
            grad_t[cols, :] = grad
            wide[0:16, cols] = dot(ones, grad, NT)
            wide[16:32, cols] = dot(slope, hidden_t[cols, :], NT)
            return carry

        lax.fori_loop(0, H // 256, backward, 0)
        pl.semaphore_wait(barrier, SHARDS)

        def dense(step, carry):
            chunk = lax.rem(step + me // 16, 4)
            rows = dot(pooled_t[part(chunk, 256), :], grad_t[...], NT).astype(BF)
            gw[part(chunk, 16)] = rows.reshape(16, PIECE, H)

            def send(step, carry):
                to = chunk * 16 + lax.rem(me + step, 16)
                pltpu.make_async_remote_copy(
                    gw.at[to], rw.at[me], sends.at[0], recvs.at[0], (1, to), MESH
                ).start()
                return carry

            lax.fori_loop(0, 16, send, 0)
            return carry

        lax.fori_loop(0, 4, dense, 0)

        def rows_grad(slot, carry):
            grad_rows[:, part(slot, N)] = dot(weight[part(slot, E), :], grad_t[...]).astype(BF)
            return carry

        lax.fori_loop(0, SLOTS, rows_grad, 0)
        for row in range(8):
            small[row : row + 1, :] = wide[0:1, row * E : (row + 1) * E]
            small[row + 8 : row + 9, :] = wide[16:17, row * E : (row + 1) * E]
        small_piece = jnp.broadcast_to(small[...].astype(BF)[None], (16, PIECE, E))

        def hot_grad(block, carry):
            rows = dot(counts[part(block, SPAN), :], grad_rows[...], NT).astype(BF)
            gh[part(block, 16), 0:PIECE, :] = rows.reshape(16, PIECE, E)
            gh[part(block, 16), PIECE : 2 * PIECE, :] = small_piece
            return carry

        lax.fori_loop(0, HOT // SPAN, hot_grad, 0)
        send_all(0, lambda to: gh.at[to], rh.at[me], sends.at[1], recvs.at[1])

        def cold_grad(block, carry):
            grad = dot(counts[pl.ds(pl.multiple_of(HOT + block * SPAN, SPAN), SPAN), :], grad_rows[...], NT)
            rows = part(block, SPAN)
            fresh = step_rows(cold[rows, :], grad)
            cold_out[rows, :] = fresh.astype(BF)
            marked = [
                jnp.where(pushed[block * (SPAN // BLK) + at] == 1, fresh[at * BLK : (at + 1) * BLK], unsent)
                for at in range(SPAN // BLK)
            ]
            learned[part(block, 8)] = jnp.concatenate(marked, axis=0).astype(BF).reshape(8, 32, E)
            return carry

        lax.fori_loop(0, COLD // SPAN, cold_grad, 0)

        def arrange(step, carry):
            outgoing[step] = learned[source[step]]
            return carry

        lax.fori_loop(0, SHARDS, arrange, 0)
        send_all(0, lambda to: outgoing.at[to], arrived.at[me], sends.at[2], recvs.at[2])
        drain(gw, sends.at[0])
        drain(gh, sends.at[1])
        drain(outgoing, sends.at[2])
        drain(weight_after, recvs.at[5])
        drain(hot_after, recvs.at[6])

    @pl.when(role == 1)
    def _():
        def count_slot(slot, carry):
            own, mult = slot_rows(ids, slot)
            lanes = part(slot, N)

            def build(block, carry):
                counts[part(block, SPAN), lanes] = count_block(own, mult, block)
                return carry

            return lax.fori_loop(0, TABLE // SPAN, build, carry)

        lax.fori_loop(0, SLOTS, count_slot, 0)
        pl.semaphore_wait(barrier, SHARDS)
        drain(rw, recvs.at[0])
        piece_w[...] = lax.fori_loop(
            0,
            SHARDS,
            lambda step, total: total + rw[step].astype(F32),
            jnp.zeros((PIECE, H), F32),
        ).astype(BF)
        send_all(1, lambda to: piece_w, allw.at[me], sends.at[0], recvs.at[3])
        allw[me] = piece_w[...]
        drain(rh, recvs.at[1])
        total = lax.fori_loop(
            0,
            SHARDS,
            lambda step, total: total + rh[step].astype(F32),
            jnp.zeros((2 * PIECE, E), F32),
        )
        piece_h[...] = step_rows(hot[part(me, PIECE), :], total[:PIECE]).astype(BF)
        send_all(1, lambda to: piece_h, allh.at[me], sends.at[1], recvs.at[4])
        allh[me] = piece_h[...]
        hot_after[...] = piece_h[...]
        sums = total[PIECE:]
        bias_sum, out_sum = sums[:8], sums[8:]
        bias_scale = 0.5 / jnp.sqrt(jnp.mean(bias_sum * bias_sum, keepdims=True) + epsilon)
        out_scale = (1.0 / math.sqrt(H)) / jnp.sqrt(jnp.mean(out_sum * out_sum, keepdims=True) + epsilon)
        small[0:8, :] = bias_sum * bias_scale
        small[8:16, :] = out_sum * out_scale
        wide[...] = jnp.zeros(wide.shape, F32)
        for row in range(8):
            wide[0:1, row * E : (row + 1) * E] = small[row : row + 1, :]
            wide[16:17, row * E : (row + 1) * E] = small[row + 8 : row + 9, :]
        bias_next = (bias[...].astype(F32) - wide[0:16, :]).astype(BF)
        out_next = (wout[...].astype(F32) - wide[16:32, :]).astype(BF)
        small16 = bias_next, out_next
        wide[0:16, :] = small16[0].astype(F32)
        wide[16:32, :] = small16[1].astype(F32)

        drain(arrived, recvs.at[2])
        eye = identity()

        def merge(block, carry):
            rows = part(block, SPAN)
            came = arrived[part(block, 8)].reshape(SPAN, E)
            fresh = jnp.where(came < unsent * 0.5, came, cold[rows, :])
            cold_out[rows, :] = fresh
            table_t[:, pl.ds(pl.multiple_of(HOT + block * SPAN, SPAN), SPAN)] = dot(eye, fresh, NT).astype(BF)
            return carry

        lax.fori_loop(0, COLD // SPAN, merge, 0)

        def pool_cold(slot, carry):
            pool_acc[part(slot, E), :] = dot(table_t[:, HOT:], counts[HOT:, part(slot, N)])
            return carry

        lax.fori_loop(0, SLOTS, pool_cold, 0)
        drain(allh.at[pl.ds(0, SHARDS - 1)], recvs.at[4])
        table_t[:, :HOT] = dot(eye, allh[...].reshape(HOT, E), NT).astype(BF)

        def pool_hot(slot, carry):
            rows = part(slot, E)
            pooled_t[rows, :] = (
                pool_acc[rows, :] + dot(table_t[:, :HOT], counts[:HOT, part(slot, N)])
            ).astype(BF)
            return carry

        lax.fori_loop(0, SLOTS, pool_hot, 0)
        drain(allw.at[pl.ds(0, SHARDS - 1)], recvs.at[3])

        def squares(step, total):
            value = allw[step].astype(F32)
            return total + value * value

        total = lax.fori_loop(0, SHARDS, squares, jnp.zeros((PIECE, H), F32))
        scale = (1.0 / math.sqrt(H)) / jnp.sqrt(jnp.sum(total, keepdims=True) / (H * H) + epsilon)

        def update(step, carry):
            rows = part(step, PIECE)
            next_w[rows, :] = (
                weight[rows, :].astype(F32) - allw[step].astype(F32) * scale
            ).astype(BF)
            return carry

        lax.fori_loop(0, SHARDS, update, 0)
        weight_after[...] = next_w[part(me, PIECE), :]
        piece_w2 = next_w.at[part(me, PIECE)]
        drain(allw.at[pl.ds(0, SHARDS - 1)], sends.at[0])
        drain(allh.at[pl.ds(0, SHARDS - 1)], sends.at[1])
        final_w = pltpu.make_async_remote_copy(
            piece_w2, weight_after, sends.at[2], recvs.at[5], (0, me), MESH
        )
        final_h = pltpu.make_async_remote_copy(
            piece_h, hot_after, sends.at[3], recvs.at[6], (0, me), MESH
        )
        final_w.start()
        final_h.start()
        ones = (lax.broadcasted_iota(jnp.int32, (16, N), 0) == 0).astype(F32).astype(BF)

        def score(chunk, logit):
            cols = part(chunk, 256)
            pre = dot(next_w[:, cols], pooled_t[...], TN) + dot(wide[0:16, cols].astype(BF), ones, TN)
            hidden = (pre * sigmoid(pre)).astype(BF)
            return logit + dot(wide[16:32, cols].astype(BF), hidden)

        scores[...] = lax.fori_loop(0, H // 256, score, jnp.zeros((16, N), F32))[0:1]
        final_w.wait_send()
        final_h.wait_send()


def run_round(ids, labels, hot, cold, weight, bias, wout, source, pushed):
    vmem = pl.BlockSpec(memory_space=pltpu.VMEM)
    smem = pl.BlockSpec(memory_space=pltpu.SMEM)
    return pl.pallas_call(
        round_kernel,
        out_shape=(
            jax.ShapeDtypeStruct((1, N), F32),
            jax.ShapeDtypeStruct((COLD, E), BF),
            jax.ShapeDtypeStruct((PIECE, E), BF),
            jax.ShapeDtypeStruct((PIECE, H), BF),
        ),
        in_specs=[vmem] * 7 + [smem] * 2,
        out_specs=(vmem,) * 4,
        scratch_shapes=[
            pltpu.VMEM((TABLE, SLOTS * N), BF),
            pltpu.VMEM((E, TABLE), BF),
            pltpu.VMEM((H, N), BF),
            pltpu.VMEM((H, N), F32),
            pltpu.VMEM((H, N), BF),
            pltpu.VMEM((H, N), BF),
            pltpu.VMEM((E, SLOTS * N), BF),
            pltpu.VMEM((H, N), F32),
            pltpu.VMEM((SHARDS, PIECE, H), BF),
            pltpu.VMEM((SHARDS, PIECE, H), BF),
            pltpu.VMEM((SHARDS, PIECE, H), BF),
            pltpu.VMEM((SHARDS, 2 * PIECE, E), BF),
            pltpu.VMEM((SHARDS, 2 * PIECE, E), BF),
            pltpu.VMEM((SHARDS, PIECE, E), BF),
            pltpu.VMEM((PIECE, H), BF),
            pltpu.VMEM((PIECE, E), BF),
            pltpu.VMEM((SHARDS, 32, E), BF),
            pltpu.VMEM((SHARDS, 32, E), BF),
            pltpu.VMEM((SHARDS, 32, E), BF),
            pltpu.VMEM((16, E), F32),
            pltpu.VMEM((32, H), F32),
            pltpu.VMEM((H, H), BF),
            pltpu.SemaphoreType.DMA((4,)),
            pltpu.SemaphoreType.DMA((7,)),
        ],
        compiler_params=pltpu.CompilerParams(
            collective_id=0, has_side_effects=True, vmem_limit_bytes=58 << 20
        ),
        name="round",
    )(ids, labels, hot, cold, weight, bias, wout, source, pushed)


def on_device(
    feature_ids, labels, cold_rows, hot_rows, block_owner, pushed, weight_in, bias_in, weight_out
):
    owner_ids = lax.broadcasted_iota(jnp.int32, (SHARDS, SHARDS), 1)
    group_ids = lax.broadcasted_iota(jnp.int32, (SHARDS, SHARDS), 0)
    owner_match = (block_owner[0][:, None] == owner_ids).astype(jnp.int32)
    source = jnp.sum(owner_match * group_ids, axis=0)
    scores, cold_out, hot_after, weight_after = run_round(
        feature_ids[0],
        labels[None],
        hot_rows,
        cold_rows[0],
        weight_in,
        jnp.pad(bias_in[None], ((0, 15), (0, 0))),
        jnp.pad(weight_out[None], ((0, 15), (0, 0))),
        source,
        pushed,
    )
    return (scores, cold_out[None], hot_after, weight_after)


def solution(mesh):
    in_specs = (
        P("role", None, None, "shard"),
        P("shard"),
        P("role", "shard", None),
        P(),
        P("shard", None),
        P("shard"),
        P(),
        P(),
        P(),
    )
    out_specs = (P("role", "shard"), P("role", "shard", None), P("shard", None), P("shard", None))
    return jax.shard_map(
        on_device, mesh=mesh, in_specs=in_specs, out_specs=out_specs, check_vma=False
    )
```

```python
import math

import jax
import jax.numpy as jnp
from jax import lax
from jax.experimental import pallas as pl
from jax.experimental.pallas import tpu as pltpu
from jax.sharding import PartitionSpec as P

row_rate = 0.25
epsilon = 1e-06
unsent = 1e30
BF = jnp.bfloat16
F32 = jnp.float32
MESH = pl.DeviceIdType.MESH
NN = (((1,), (0,)), ((), ()))
NT = (((1,), (1,)), ((), ()))
TN = (((0,), (0,)), ((), ()))

SHARDS = 64
SLOTS = 8
BAGS = 4
N = 512
E = 128
H = 1024
HOT = 1024
COLD = 2048
TABLE = HOT + COLD
PIECE = H // SHARDS
BLK = 8
SPAN = 256


def dot(lhs, rhs, dims=NN):
    return lax.dot_general(lhs, rhs, dims, preferred_element_type=F32)


def sigmoid(value):
    return 0.5 * jnp.tanh(0.5 * value) + 0.5


def step_rows(old_rows, grad_rows):
    scale_rows = jnp.sqrt(jnp.mean(grad_rows * grad_rows, axis=-1, keepdims=True) + epsilon)
    return old_rows.astype(F32) - row_rate * grad_rows / scale_rows


def part(index, size):
    return pl.ds(pl.multiple_of(index * size, size), size)


def identity():
    rows = lax.broadcasted_iota(jnp.int32, (E, E), 0)
    return (rows == lax.broadcasted_iota(jnp.int32, (E, E), 1)).astype(F32).astype(BF)


def first_row(value):
    return lax.broadcasted_iota(jnp.int32, (16, N), 0) == 0


def slot_rows(ids, slot):
    own = [ids[slot, bag][None, :] for bag in range(BAGS)]
    mult = [sum((one == other).astype(F32) for other in own).astype(BF) for one in own]
    return own, mult


def count_block(own, mult, block):
    spots = lax.broadcasted_iota(jnp.int32, (SPAN, N), 0).astype(F32).astype(BF)
    acc = jnp.zeros((SPAN, N), BF)
    for bag in range(BAGS):
        at = jnp.clip(own[bag] - block * SPAN, -1, SPAN).astype(F32).astype(BF)
        acc = jnp.where(spots == at, mult[bag], acc)
    return acc


def round_kernel(
    ids, labels, hot, cold, weight, bias_in, weight_out, owner, pushed,
    scores, cold_out, hot_after, weight_after,
    counts, table_t, pooled_t, pre_t, hidden_t, grad_t, grad_rows, pool_acc,
    gw, rw, allw, gh, rh, allh, piece_w, piece_h, learned, outgoing, arrived, small, wide,
    next_w, bias, wout, source_rows, source, sends, recvs, local,
):
    role = lax.axis_index("role")
    me = lax.axis_index("shard")
    barrier = pltpu.get_barrier_semaphore()
    top = lax.broadcasted_iota(jnp.int32, (16, H), 0) == 0
    bias[...] = jnp.where(top, bias_in[...].reshape(1, H).astype(F32), 0.0).astype(BF)
    wout[...] = jnp.where(top, weight_out[...].reshape(1, H).astype(F32), 0.0).astype(BF)

    def send_all(lo, source_of, target, sem_out, sem_in):
        def body(step, carry):
            to = lax.rem(me + step, SHARDS)
            pltpu.make_async_remote_copy(
                source_of(to), target, sem_out, sem_in, (1, to), MESH
            ).start()
            return carry

        lax.fori_loop(lo, SHARDS, body, 0)

    def drain(ref, sem):
        pltpu.make_async_copy(ref, ref, sem).wait()

    @pl.when(role == 1)
    def _():
        def greet(step, carry):
            pl.semaphore_signal(barrier, inc=1, device_id=(0, step), device_id_type=MESH)

            @pl.when(step != me)
            def _():
                pl.semaphore_signal(barrier, inc=1, device_id=(1, step), device_id_type=MESH)

            return carry

        lax.fori_loop(0, SHARDS, greet, 0)

    @pl.when(role == 0)
    def _():
        pl.semaphore_signal(barrier, inc=1, device_id=(1, me), device_id_type=MESH)
        groups = lax.broadcasted_iota(jnp.int32, (SHARDS, SHARDS), 1)
        owners = lax.broadcasted_iota(jnp.int32, (SHARDS, SHARDS), 0)
        found = jnp.where(owner[...] == owners, groups, 0)
        spot = jnp.clip(jnp.sum(found, axis=1, keepdims=True), 0, SHARDS - 1)
        source_rows[...] = jnp.broadcast_to(spot, (SHARDS, E))
        fetch = pltpu.make_async_copy(source_rows, source, local.at[0])
        fetch.start()
        eye = identity()
        table_t[:, :HOT] = dot(eye, hot[...], NT).astype(BF)
        table_t[:, HOT:] = dot(eye, cold[...], NT).astype(BF)

        def pool_slot(slot, carry):
            own, mult = slot_rows(ids, slot)
            lanes = part(slot, N)

            def build(block, carry):
                counts[part(block, SPAN), lanes] = count_block(own, mult, block)
                return carry

            lax.fori_loop(0, TABLE // SPAN, build, 0)
            pooled_t[part(slot, E), :] = dot(table_t[...], counts[:, lanes]).astype(BF)
            return carry

        lax.fori_loop(0, SLOTS, pool_slot, 0)
        first = lax.broadcasted_iota(jnp.int32, (16, N), 0) == 0
        ones = first.astype(F32).astype(BF)

        def forward(chunk, logit):
            cols = part(chunk, 256)
            pre = dot(weight[:, cols], pooled_t[...], TN) + dot(bias[:, cols], ones, TN)
            pre_t[cols, :] = pre
            hidden = (pre * sigmoid(pre)).astype(BF)
            hidden_t[cols, :] = hidden
            return logit + dot(wout[:, cols], hidden)

        logit = lax.fori_loop(0, H // 256, forward, jnp.zeros((16, N), F32))
        scores[...] = logit[0:1]
        slope = jnp.where(first, sigmoid(logit) - labels[...].reshape(1, N), 0.0).astype(BF)

        def backward(chunk, carry):
            cols = part(chunk, 256)
            pre = pre_t[cols, :]
            gate = sigmoid(pre)
            grad = (dot(wout[:, cols], slope, TN) * (gate * (1.0 + pre * (1.0 - gate)))).astype(BF)
            grad_t[cols, :] = grad
            wide[0:16, cols] = dot(ones, grad, NT)
            wide[16:32, cols] = dot(slope, hidden_t[cols, :], NT)
            return carry

        lax.fori_loop(0, H // 256, backward, 0)
        pl.semaphore_wait(barrier, SHARDS)

        def dense(step, carry):
            chunk = lax.rem(step + me // 16, 4)
            rows = dot(pooled_t[part(chunk, 256), :], grad_t[...], NT).astype(BF)
            gw[part(chunk, 16)] = rows.reshape(16, PIECE, H)

            def send(step, carry):
                to = chunk * 16 + lax.rem(me + step, 16)
                pltpu.make_async_remote_copy(
                    gw.at[to], rw.at[me], sends.at[0], recvs.at[0], (1, to), MESH
                ).start()
                return carry

            lax.fori_loop(0, 16, send, 0)
            return carry

        lax.fori_loop(0, 4, dense, 0)

        def rows_grad(slot, carry):
            grad_rows[:, part(slot, N)] = dot(weight[part(slot, E), :], grad_t[...]).astype(BF)
            return carry

        lax.fori_loop(0, SLOTS, rows_grad, 0)
        for row in range(8):
            small[row : row + 1, :] = wide[0:1, row * E : (row + 1) * E]
            small[row + 8 : row + 9, :] = wide[16:17, row * E : (row + 1) * E]
        small_piece = jnp.broadcast_to(small[...].astype(BF)[None], (16, PIECE, E))

        def hot_grad(block, carry):
            rows = dot(counts[part(block, SPAN), :], grad_rows[...], NT).astype(BF)
            gh[part(block, 16), 0:PIECE, :] = rows.reshape(16, PIECE, E)
            gh[part(block, 16), PIECE : 2 * PIECE, :] = small_piece
            return carry

        lax.fori_loop(0, HOT // SPAN, hot_grad, 0)
        send_all(0, lambda to: gh.at[to], rh.at[me], sends.at[1], recvs.at[1])

        def cold_grad(block, carry):
            grad = dot(counts[pl.ds(pl.multiple_of(HOT + block * SPAN, SPAN), SPAN), :], grad_rows[...], NT)
            rows = part(block, SPAN)
            fresh = step_rows(cold[rows, :], grad)
            cold_out[rows, :] = fresh.astype(BF)
            marked = [
                jnp.where(pushed[block * (SPAN // BLK) + at] == 1, fresh[at * BLK : (at + 1) * BLK], unsent)
                for at in range(SPAN // BLK)
            ]
            learned[part(block, 8)] = jnp.concatenate(marked, axis=0).astype(BF).reshape(8, 32, E)
            return carry

        lax.fori_loop(0, COLD // SPAN, cold_grad, 0)

        fetch.wait()

        def arrange(step, carry):
            outgoing[step] = learned[jnp.clip(source[step, 0], 0, SHARDS - 1)]
            return carry

        lax.fori_loop(0, SHARDS, arrange, 0)
        send_all(0, lambda to: outgoing.at[to], arrived.at[me], sends.at[2], recvs.at[2])
        drain(gw, sends.at[0])
        drain(gh, sends.at[1])
        drain(outgoing, sends.at[2])
        drain(weight_after, recvs.at[5])
        drain(hot_after, recvs.at[6])

    @pl.when(role == 1)
    def _():
        def count_slot(slot, carry):
            own, mult = slot_rows(ids, slot)
            lanes = part(slot, N)

            def build(block, carry):
                counts[part(block, SPAN), lanes] = count_block(own, mult, block)
                return carry

            return lax.fori_loop(0, TABLE // SPAN, build, carry)

        lax.fori_loop(0, SLOTS, count_slot, 0)
        pl.semaphore_wait(barrier, SHARDS)
        drain(rw, recvs.at[0])
        piece_w[...] = lax.fori_loop(
            0,
            SHARDS,
            lambda step, total: total + rw[step].astype(F32),
            jnp.zeros((PIECE, H), F32),
        ).astype(BF)
        send_all(1, lambda to: piece_w, allw.at[me], sends.at[0], recvs.at[3])
        allw[me] = piece_w[...]
        drain(rh, recvs.at[1])
        total = lax.fori_loop(
            0,
            SHARDS,
            lambda step, total: total + rh[step].astype(F32),
            jnp.zeros((2 * PIECE, E), F32),
        )
        piece_h[...] = step_rows(hot[part(me, PIECE), :], total[:PIECE]).astype(BF)
        send_all(1, lambda to: piece_h, allh.at[me], sends.at[1], recvs.at[4])
        allh[me] = piece_h[...]
        hot_after[...] = piece_h[...]
        sums = total[PIECE:]
        bias_sum, out_sum = sums[:8], sums[8:]
        bias_scale = 0.5 / jnp.sqrt(jnp.mean(bias_sum * bias_sum, keepdims=True) + epsilon)
        out_scale = (1.0 / math.sqrt(H)) / jnp.sqrt(jnp.mean(out_sum * out_sum, keepdims=True) + epsilon)
        small[0:8, :] = bias_sum * bias_scale
        small[8:16, :] = out_sum * out_scale
        wide[...] = jnp.zeros(wide.shape, F32)
        for row in range(8):
            wide[0:1, row * E : (row + 1) * E] = small[row : row + 1, :]
            wide[16:17, row * E : (row + 1) * E] = small[row + 8 : row + 9, :]
        bias_next = (bias[...].astype(F32) - wide[0:16, :]).astype(BF)
        out_next = (wout[...].astype(F32) - wide[16:32, :]).astype(BF)
        small16 = bias_next, out_next
        wide[0:16, :] = small16[0].astype(F32)
        wide[16:32, :] = small16[1].astype(F32)

        drain(arrived, recvs.at[2])
        eye = identity()

        def merge(block, carry):
            rows = part(block, SPAN)
            came = arrived[part(block, 8)].reshape(SPAN, E)
            fresh = jnp.where(came < unsent * 0.5, came, cold[rows, :])
            cold_out[rows, :] = fresh
            table_t[:, pl.ds(pl.multiple_of(HOT + block * SPAN, SPAN), SPAN)] = dot(eye, fresh, NT).astype(BF)
            return carry

        lax.fori_loop(0, COLD // SPAN, merge, 0)

        def pool_cold(slot, carry):
            pool_acc[part(slot, E), :] = dot(table_t[:, HOT:], counts[HOT:, part(slot, N)])
            return carry

        lax.fori_loop(0, SLOTS, pool_cold, 0)
        drain(allh.at[pl.ds(0, SHARDS - 1)], recvs.at[4])
        table_t[:, :HOT] = dot(eye, allh[...].reshape(HOT, E), NT).astype(BF)

        def pool_hot(slot, carry):
            rows = part(slot, E)
            pooled_t[rows, :] = (
                pool_acc[rows, :] + dot(table_t[:, :HOT], counts[:HOT, part(slot, N)])
            ).astype(BF)
            return carry

        lax.fori_loop(0, SLOTS, pool_hot, 0)
        drain(allw.at[pl.ds(0, SHARDS - 1)], recvs.at[3])

        def squares(step, total):
            value = allw[step].astype(F32)
            return total + value * value

        total = lax.fori_loop(0, SHARDS, squares, jnp.zeros((PIECE, H), F32))
        scale = (1.0 / math.sqrt(H)) / jnp.sqrt(jnp.sum(total, keepdims=True) / (H * H) + epsilon)

        def update(step, carry):
            rows = part(step, PIECE)
            next_w[rows, :] = (
                weight[rows, :].astype(F32) - allw[step].astype(F32) * scale
            ).astype(BF)
            return carry

        lax.fori_loop(0, SHARDS, update, 0)
        weight_after[...] = next_w[part(me, PIECE), :]
        piece_w2 = next_w.at[part(me, PIECE)]
        drain(allw.at[pl.ds(0, SHARDS - 1)], sends.at[0])
        drain(allh.at[pl.ds(0, SHARDS - 1)], sends.at[1])
        final_w = pltpu.make_async_remote_copy(
            piece_w2, weight_after, sends.at[2], recvs.at[5], (0, me), MESH
        )
        final_h = pltpu.make_async_remote_copy(
            piece_h, hot_after, sends.at[3], recvs.at[6], (0, me), MESH
        )
        final_w.start()
        final_h.start()
        ones = (lax.broadcasted_iota(jnp.int32, (16, N), 0) == 0).astype(F32).astype(BF)

        def score(chunk, logit):
            cols = part(chunk, 256)
            pre = dot(next_w[:, cols], pooled_t[...], TN) + dot(wide[0:16, cols].astype(BF), ones, TN)
            hidden = (pre * sigmoid(pre)).astype(BF)
            return logit + dot(wide[16:32, cols].astype(BF), hidden)

        scores[...] = lax.fori_loop(0, H // 256, score, jnp.zeros((16, N), F32))[0:1]
        final_w.wait_send()
        final_h.wait_send()


def run_round(ids, labels, hot, cold, weight, bias, wout, owner, pushed):
    vmem = pl.BlockSpec(memory_space=pltpu.VMEM)
    smem = pl.BlockSpec(memory_space=pltpu.SMEM)
    return pl.pallas_call(
        round_kernel,
        out_shape=(
            jax.ShapeDtypeStruct((1, N), F32),
            jax.ShapeDtypeStruct((COLD, E), BF),
            jax.ShapeDtypeStruct((PIECE, E), BF),
            jax.ShapeDtypeStruct((PIECE, H), BF),
        ),
        in_specs=[vmem] * 8 + [smem],
        out_specs=(vmem,) * 4,
        scratch_shapes=[
            pltpu.VMEM((TABLE, SLOTS * N), BF),
            pltpu.VMEM((E, TABLE), BF),
            pltpu.VMEM((H, N), BF),
            pltpu.VMEM((H, N), F32),
            pltpu.VMEM((H, N), BF),
            pltpu.VMEM((H, N), BF),
            pltpu.VMEM((E, SLOTS * N), BF),
            pltpu.VMEM((H, N), F32),
            pltpu.VMEM((SHARDS, PIECE, H), BF),
            pltpu.VMEM((SHARDS, PIECE, H), BF),
            pltpu.VMEM((SHARDS, PIECE, H), BF),
            pltpu.VMEM((SHARDS, 2 * PIECE, E), BF),
            pltpu.VMEM((SHARDS, 2 * PIECE, E), BF),
            pltpu.VMEM((SHARDS, PIECE, E), BF),
            pltpu.VMEM((PIECE, H), BF),
            pltpu.VMEM((PIECE, E), BF),
            pltpu.VMEM((SHARDS, 32, E), BF),
            pltpu.VMEM((SHARDS, 32, E), BF),
            pltpu.VMEM((SHARDS, 32, E), BF),
            pltpu.VMEM((16, E), F32),
            pltpu.VMEM((32, H), F32),
            pltpu.VMEM((H, H), BF),
            pltpu.VMEM((16, H), BF),
            pltpu.VMEM((16, H), BF),
            pltpu.VMEM((SHARDS, E), jnp.int32),
            pltpu.SMEM((SHARDS, E), jnp.int32),
            pltpu.SemaphoreType.DMA((4,)),
            pltpu.SemaphoreType.DMA((7,)),
            pltpu.SemaphoreType.DMA((1,)),
        ],
        compiler_params=pltpu.CompilerParams(
            collective_id=0, has_side_effects=True, vmem_limit_bytes=58 << 20
        ),
        name="round",
    )(ids, labels, hot, cold, weight, bias, wout, owner, pushed)


def hand_over_kernel(*refs):
    count = len(refs) // 2
    copies = [
        pltpu.make_async_copy(refs[at], refs[count + at], refs[-1].at[at]) for at in range(count)
    ]
    for copy in copies:
        copy.start()
    for copy in copies:
        copy.wait()


def hand_over(arrays):
    return pl.pallas_call(
        hand_over_kernel,
        out_shape=tuple(jax.ShapeDtypeStruct(array.shape, array.dtype) for array in arrays),
        in_specs=[pl.BlockSpec(memory_space=pl.ANY)] * len(arrays),
        out_specs=(pl.BlockSpec(memory_space=pl.ANY),) * len(arrays),
        scratch_shapes=[pltpu.SemaphoreType.DMA((len(arrays),))],
        name="hand_over",
    )(*arrays)


def on_device(
    feature_ids, labels, cold_rows, hot_rows, block_owner, pushed, weight_in, bias_in, weight_out
):
    scores, cold_out, hot_after, weight_after = hand_over(
        run_round(
            feature_ids[0],
            labels,
            hot_rows,
            cold_rows[0],
            weight_in,
            bias_in,
            weight_out,
            block_owner,
            pushed,
        )
    )
    return (scores, cold_out[None], hot_after, weight_after)


def solution(mesh):
    in_specs = (
        P("role", None, None, "shard"),
        P("shard"),
        P("role", "shard", None),
        P(),
        P("shard", None),
        P("shard"),
        P(),
        P(),
        P(),
    )
    out_specs = (P("role", "shard"), P("role", "shard", None), P("shard", None), P("shard", None))
    return jax.shard_map(
        on_device, mesh=mesh, in_specs=in_specs, out_specs=out_specs, check_vma=False
    )
```

```python
import math

import jax
import jax.numpy as jnp
from jax import lax
from jax.experimental import pallas as pl
from jax.experimental.pallas import tpu as pltpu
from jax.sharding import PartitionSpec as P

row_rate = 0.25
epsilon = 1e-06
unsent = 1e30
BF = jnp.bfloat16
F32 = jnp.float32
MESH = pl.DeviceIdType.MESH
NN = (((1,), (0,)), ((), ()))
NT = (((1,), (1,)), ((), ()))
TN = (((0,), (0,)), ((), ()))

SHARDS = 64
SLOTS = 8
BAGS = 4
N = 512
E = 128
H = 1024
HOT = 1024
COLD = 2048
TABLE = HOT + COLD
PIECE = H // SHARDS
BLK = 8
SPAN = 256


def dot(lhs, rhs, dims=NN):
    return lax.dot_general(lhs, rhs, dims, preferred_element_type=F32)


def sigmoid(value):
    return 0.5 * jnp.tanh(0.5 * value) + 0.5


def step_rows(old_rows, grad_rows):
    scale_rows = jnp.sqrt(jnp.mean(grad_rows * grad_rows, axis=-1, keepdims=True) + epsilon)
    return old_rows.astype(F32) - row_rate * grad_rows / scale_rows


def part(index, size):
    return pl.ds(pl.multiple_of(index * size, size), size)


def identity():
    rows = lax.broadcasted_iota(jnp.int32, (E, E), 0)
    return (rows == lax.broadcasted_iota(jnp.int32, (E, E), 1)).astype(F32).astype(BF)


def first_row(value):
    return lax.broadcasted_iota(jnp.int32, (16, N), 0) == 0


def slot_rows(ids, slot):
    own = [ids[slot, bag][None, :] for bag in range(BAGS)]
    mult = [sum((one == other).astype(F32) for other in own).astype(BF) for one in own]
    return own, mult


def count_block(own, mult, block):
    spots = lax.broadcasted_iota(jnp.int32, (SPAN, N), 0).astype(F32).astype(BF)
    acc = jnp.zeros((SPAN, N), BF)
    for bag in range(BAGS):
        at = jnp.clip(own[bag] - block * SPAN, -1, SPAN).astype(F32).astype(BF)
        acc = jnp.where(spots == at, mult[bag], acc)
    return acc


def round_kernel(
    ids, labels, hot, cold, weight, bias_in, weight_out, owner, pushed,
    scores, cold_out, hot_after, weight_after,
    counts, table_t, pooled_t, pre_t, hidden_t, grad_t, grad_rows, pool_acc,
    gw, rw, allw, gh, rh, allh, piece_w, piece_h, learned, outgoing, arrived, small, wide,
    next_w, bias, wout, source_rows, source, sends, recvs, local,
):
    role = lax.axis_index("role")
    me = lax.axis_index("shard")
    barrier = pltpu.get_barrier_semaphore()
    top = lax.broadcasted_iota(jnp.int32, (16, H), 0) == 0
    bias[...] = jnp.where(top, bias_in[...].reshape(1, H).astype(F32), 0.0).astype(BF)
    wout[...] = jnp.where(top, weight_out[...].reshape(1, H).astype(F32), 0.0).astype(BF)

    def send_all(lo, source_of, target, sem_out, sem_in):
        def body(step, carry):
            to = lax.rem(me + step, SHARDS)
            pltpu.make_async_remote_copy(
                source_of(to), target, sem_out, sem_in, (1, to), MESH
            ).start()
            return carry

        lax.fori_loop(lo, SHARDS, body, 0)

    def drain(ref, sem):
        pltpu.make_async_copy(ref, ref, sem).wait()

    @pl.when(role == 1)
    def _():
        def greet(step, carry):
            pl.semaphore_signal(barrier, inc=1, device_id=(0, step), device_id_type=MESH)

            @pl.when(step != me)
            def _():
                pl.semaphore_signal(barrier, inc=1, device_id=(1, step), device_id_type=MESH)

            return carry

        lax.fori_loop(0, SHARDS, greet, 0)

    @pl.when(role == 0)
    def _():
        pl.semaphore_signal(barrier, inc=1, device_id=(1, me), device_id_type=MESH)
        groups = lax.broadcasted_iota(jnp.int32, (SHARDS, SHARDS), 1)
        owners = lax.broadcasted_iota(jnp.int32, (SHARDS, SHARDS), 0)
        found = jnp.where(owner[...] == owners, groups, 0)
        spot = jnp.clip(jnp.sum(found, axis=1, keepdims=True), 0, SHARDS - 1)
        source_rows[...] = jnp.broadcast_to(spot, (SHARDS, E))
        fetch = pltpu.make_async_copy(source_rows, source, local.at[0])
        fetch.start()
        eye = identity()
        table_t[:, :HOT] = dot(eye, hot[...], NT).astype(BF)
        table_t[:, HOT:] = dot(eye, cold[...], NT).astype(BF)

        def pool_slot(slot, carry):
            own, mult = slot_rows(ids, slot)
            lanes = part(slot, N)

            def build(block, carry):
                counts[part(block, SPAN), lanes] = count_block(own, mult, block)
                return carry

            lax.fori_loop(0, TABLE // SPAN, build, 0)
            pooled_t[part(slot, E), :] = dot(table_t[...], counts[:, lanes]).astype(BF)
            return carry

        lax.fori_loop(0, SLOTS, pool_slot, 0)
        first = lax.broadcasted_iota(jnp.int32, (16, N), 0) == 0
        ones = first.astype(F32).astype(BF)

        def forward(chunk, logit):
            cols = part(chunk, 256)
            pre = dot(weight[:, cols], pooled_t[...], TN) + dot(bias[:, cols], ones, TN)
            pre_t[cols, :] = pre
            hidden = (pre * sigmoid(pre)).astype(BF)
            hidden_t[cols, :] = hidden
            return logit + dot(wout[:, cols], hidden)

        logit = lax.fori_loop(0, H // 256, forward, jnp.zeros((16, N), F32))
        scores[...] = logit[0:1]
        slope = jnp.where(first, sigmoid(logit) - labels[...].reshape(1, N), 0.0).astype(BF)

        def backward(chunk, carry):
            cols = part(chunk, 256)
            pre = pre_t[cols, :]
            gate = sigmoid(pre)
            grad = (dot(wout[:, cols], slope, TN) * (gate * (1.0 + pre * (1.0 - gate)))).astype(BF)
            grad_t[cols, :] = grad
            wide[0:16, cols] = dot(ones, grad, NT)
            wide[16:32, cols] = dot(slope, hidden_t[cols, :], NT)
            return carry

        lax.fori_loop(0, H // 256, backward, 0)
        pl.semaphore_wait(barrier, SHARDS)

        def dense(step, carry):
            chunk = lax.rem(step + me // 16, 4)
            rows = dot(pooled_t[part(chunk, 256), :], grad_t[...], NT).astype(BF)
            gw[part(chunk, 16)] = rows.reshape(16, PIECE, H)

            def send(step, carry):
                to = chunk * 16 + lax.rem(me + step, 16)
                pltpu.make_async_remote_copy(
                    gw.at[to], rw.at[me], sends.at[0], recvs.at[0], (1, to), MESH
                ).start()
                return carry

            lax.fori_loop(0, 16, send, 0)
            return carry

        lax.fori_loop(0, 4, dense, 0)

        def rows_grad(slot, carry):
            grad_rows[:, part(slot, N)] = dot(weight[part(slot, E), :], grad_t[...]).astype(BF)
            return carry

        lax.fori_loop(0, SLOTS, rows_grad, 0)
        for row in range(8):
            small[row : row + 1, :] = wide[0:1, row * E : (row + 1) * E]
            small[row + 8 : row + 9, :] = wide[16:17, row * E : (row + 1) * E]
        small_piece = jnp.broadcast_to(small[...].astype(BF)[None], (16, PIECE, E))

        def hot_grad(block, carry):
            rows = dot(counts[part(block, SPAN), :], grad_rows[...], NT).astype(BF)
            gh[part(block, 16), 0:PIECE, :] = rows.reshape(16, PIECE, E)
            gh[part(block, 16), PIECE : 2 * PIECE, :] = small_piece
            return carry

        lax.fori_loop(0, HOT // SPAN, hot_grad, 0)
        send_all(0, lambda to: gh.at[to], rh.at[me], sends.at[1], recvs.at[1])

        def cold_grad(block, carry):
            grad = dot(counts[pl.ds(pl.multiple_of(HOT + block * SPAN, SPAN), SPAN), :], grad_rows[...], NT)
            rows = part(block, SPAN)
            fresh = step_rows(cold[rows, :], grad)
            cold_out[rows, :] = fresh.astype(BF)
            marked = [
                jnp.where(pushed[block * (SPAN // BLK) + at] == 1, fresh[at * BLK : (at + 1) * BLK], unsent)
                for at in range(SPAN // BLK)
            ]
            learned[part(block, 8)] = jnp.concatenate(marked, axis=0).astype(BF).reshape(8, 32, E)
            return carry

        lax.fori_loop(0, COLD // SPAN, cold_grad, 0)

        fetch.wait()

        def arrange(step, carry):
            outgoing[step] = learned[jnp.clip(source[step, 0], 0, SHARDS - 1)]
            return carry

        lax.fori_loop(0, SHARDS, arrange, 0)
        send_all(0, lambda to: outgoing.at[to], arrived.at[me], sends.at[2], recvs.at[2])
        drain(gw, sends.at[0])
        drain(gh, sends.at[1])
        drain(outgoing, sends.at[2])
        drain(weight_after, recvs.at[5])
        drain(hot_after, recvs.at[6])

    @pl.when(role == 1)
    def _():
        def count_slot(slot, carry):
            own, mult = slot_rows(ids, slot)
            lanes = part(slot, N)

            def build(block, carry):
                counts[part(block, SPAN), lanes] = count_block(own, mult, block)
                return carry

            return lax.fori_loop(0, TABLE // SPAN, build, carry)

        lax.fori_loop(0, SLOTS, count_slot, 0)
        pl.semaphore_wait(barrier, SHARDS)
        drain(rw, recvs.at[0])
        piece_w[...] = lax.fori_loop(
            0,
            SHARDS,
            lambda step, total: total + rw[step].astype(F32),
            jnp.zeros((PIECE, H), F32),
        ).astype(BF)
        send_all(1, lambda to: piece_w, allw.at[me], sends.at[0], recvs.at[3])
        allw[me] = piece_w[...]
        drain(rh, recvs.at[1])
        total = lax.fori_loop(
            0,
            SHARDS,
            lambda step, total: total + rh[step].astype(F32),
            jnp.zeros((2 * PIECE, E), F32),
        )
        piece_h[...] = step_rows(hot[part(me, PIECE), :], total[:PIECE]).astype(BF)
        send_all(1, lambda to: piece_h, allh.at[me], sends.at[1], recvs.at[4])
        allh[me] = piece_h[...]
        hot_after[...] = piece_h[...]
        sums = total[PIECE:]
        bias_sum, out_sum = sums[:8], sums[8:]
        bias_scale = 0.5 / jnp.sqrt(jnp.mean(bias_sum * bias_sum, keepdims=True) + epsilon)
        out_scale = (1.0 / math.sqrt(H)) / jnp.sqrt(jnp.mean(out_sum * out_sum, keepdims=True) + epsilon)
        small[0:8, :] = bias_sum * bias_scale
        small[8:16, :] = out_sum * out_scale
        wide[...] = jnp.zeros(wide.shape, F32)
        for row in range(8):
            wide[0:1, row * E : (row + 1) * E] = small[row : row + 1, :]
            wide[16:17, row * E : (row + 1) * E] = small[row + 8 : row + 9, :]
        bias_next = (bias[...].astype(F32) - wide[0:16, :]).astype(BF)
        out_next = (wout[...].astype(F32) - wide[16:32, :]).astype(BF)
        small16 = bias_next, out_next
        wide[0:16, :] = small16[0].astype(F32)
        wide[16:32, :] = small16[1].astype(F32)

        drain(arrived, recvs.at[2])
        eye = identity()

        def merge(block, carry):
            rows = part(block, SPAN)
            came = arrived[part(block, 8)].reshape(SPAN, E)
            fresh = jnp.where(came < unsent * 0.5, came, cold[rows, :])
            cold_out[rows, :] = fresh
            table_t[:, pl.ds(pl.multiple_of(HOT + block * SPAN, SPAN), SPAN)] = dot(eye, fresh, NT).astype(BF)
            return carry

        lax.fori_loop(0, COLD // SPAN, merge, 0)

        def pool_cold(slot, carry):
            pool_acc[part(slot, E), :] = dot(table_t[:, HOT:], counts[HOT:, part(slot, N)])
            return carry

        lax.fori_loop(0, SLOTS, pool_cold, 0)
        drain(allh.at[pl.ds(0, SHARDS - 1)], recvs.at[4])
        table_t[:, :HOT] = dot(eye, allh[...].reshape(HOT, E), NT).astype(BF)

        def pool_hot(slot, carry):
            rows = part(slot, E)
            pooled_t[rows, :] = (
                pool_acc[rows, :] + dot(table_t[:, :HOT], counts[:HOT, part(slot, N)])
            ).astype(BF)
            return carry

        lax.fori_loop(0, SLOTS, pool_hot, 0)
        drain(allw.at[pl.ds(0, SHARDS - 1)], recvs.at[3])

        def squares(step, total):
            value = allw[step].astype(F32)
            return total + value * value

        total = lax.fori_loop(0, SHARDS, squares, jnp.zeros((PIECE, H), F32))
        scale = (1.0 / math.sqrt(H)) / jnp.sqrt(jnp.sum(total, keepdims=True) / (H * H) + epsilon)

        def update(step, carry):
            rows = part(step, PIECE)
            next_w[rows, :] = (
                weight[rows, :].astype(F32) - allw[step].astype(F32) * scale
            ).astype(BF)
            return carry

        lax.fori_loop(0, SHARDS, update, 0)
        weight_after[...] = next_w[part(me, PIECE), :]
        piece_w2 = next_w.at[part(me, PIECE)]
        drain(allw.at[pl.ds(0, SHARDS - 1)], sends.at[0])
        drain(allh.at[pl.ds(0, SHARDS - 1)], sends.at[1])
        final_w = pltpu.make_async_remote_copy(
            piece_w2, weight_after, sends.at[2], recvs.at[5], (0, me), MESH
        )
        final_h = pltpu.make_async_remote_copy(
            piece_h, hot_after, sends.at[3], recvs.at[6], (0, me), MESH
        )
        final_w.start()
        final_h.start()
        ones = (lax.broadcasted_iota(jnp.int32, (16, N), 0) == 0).astype(F32).astype(BF)

        def score(chunk, logit):
            cols = part(chunk, 256)
            pre = dot(next_w[:, cols], pooled_t[...], TN) + dot(wide[0:16, cols].astype(BF), ones, TN)
            hidden = (pre * sigmoid(pre)).astype(BF)
            return logit + dot(wide[16:32, cols].astype(BF), hidden)

        scores[...] = lax.fori_loop(0, H // 256, score, jnp.zeros((16, N), F32))[0:1]
        final_w.wait_send()
        final_h.wait_send()


def run_round(ids, labels, hot, cold, weight, bias, wout, owner, pushed):
    vmem = pl.BlockSpec(memory_space=pltpu.VMEM)
    smem = pl.BlockSpec(memory_space=pltpu.SMEM)
    return pl.pallas_call(
        round_kernel,
        out_shape=(
            jax.ShapeDtypeStruct((1, N), F32),
            jax.ShapeDtypeStruct((COLD, E), BF),
            jax.ShapeDtypeStruct((PIECE, E), BF),
            jax.ShapeDtypeStruct((PIECE, H), BF),
        ),
        in_specs=[vmem] * 8 + [smem],
        out_specs=(vmem,) * 4,
        scratch_shapes=[
            pltpu.VMEM((TABLE, SLOTS * N), BF),
            pltpu.VMEM((E, TABLE), BF),
            pltpu.VMEM((H, N), BF),
            pltpu.VMEM((H, N), F32),
            pltpu.VMEM((H, N), BF),
            pltpu.VMEM((H, N), BF),
            pltpu.VMEM((E, SLOTS * N), BF),
            pltpu.VMEM((H, N), F32),
            pltpu.VMEM((SHARDS, PIECE, H), BF),
            pltpu.VMEM((SHARDS, PIECE, H), BF),
            pltpu.VMEM((SHARDS, PIECE, H), BF),
            pltpu.VMEM((SHARDS, 2 * PIECE, E), BF),
            pltpu.VMEM((SHARDS, 2 * PIECE, E), BF),
            pltpu.VMEM((SHARDS, PIECE, E), BF),
            pltpu.VMEM((PIECE, H), BF),
            pltpu.VMEM((PIECE, E), BF),
            pltpu.VMEM((SHARDS, 32, E), BF),
            pltpu.VMEM((SHARDS, 32, E), BF),
            pltpu.VMEM((SHARDS, 32, E), BF),
            pltpu.VMEM((16, E), F32),
            pltpu.VMEM((32, H), F32),
            pltpu.VMEM((H, H), BF),
            pltpu.VMEM((16, H), BF),
            pltpu.VMEM((16, H), BF),
            pltpu.VMEM((SHARDS, E), jnp.int32),
            pltpu.SMEM((SHARDS, E), jnp.int32),
            pltpu.SemaphoreType.DMA((4,)),
            pltpu.SemaphoreType.DMA((7,)),
            pltpu.SemaphoreType.DMA((1,)),
        ],
        compiler_params=pltpu.CompilerParams(
            collective_id=0, has_side_effects=True, vmem_limit_bytes=58 << 20
        ),
        name="round",
    )(ids, labels, hot, cold, weight, bias, wout, owner, pushed)


def hand_over_kernel(*refs):
    count = len(refs) // 2
    copies = [
        pltpu.make_async_copy(refs[at], refs[count + at], refs[-1].at[at]) for at in range(count)
    ]
    for copy in copies:
        copy.start()
    for copy in copies:
        copy.wait()


def hand_over(arrays):
    return pl.pallas_call(
        hand_over_kernel,
        out_shape=tuple(jax.ShapeDtypeStruct(array.shape, array.dtype) for array in arrays),
        in_specs=[pl.BlockSpec(memory_space=pl.ANY)] * len(arrays),
        out_specs=(pl.BlockSpec(memory_space=pltpu.VMEM),) * len(arrays),
        scratch_shapes=[pltpu.SemaphoreType.DMA((len(arrays),))],
        name="hand_over",
    )(*arrays)


def on_device(
    feature_ids, labels, cold_rows, hot_rows, block_owner, pushed, weight_in, bias_in, weight_out
):
    scores, cold_out, hot_after, weight_after = hand_over(
        run_round(
            feature_ids[0],
            labels,
            hot_rows,
            cold_rows[0],
            weight_in,
            bias_in,
            weight_out,
            block_owner,
            pushed,
        )
    )
    return (scores, cold_out[None], hot_after, weight_after)


def solution(mesh):
    in_specs = (
        P("role", None, None, "shard"),
        P("shard"),
        P("role", "shard", None),
        P(),
        P("shard", None),
        P("shard"),
        P(),
        P(),
        P(),
    )
    out_specs = (P("role", "shard"), P("role", "shard", None), P("shard", None), P("shard", None))
    return jax.shard_map(
        on_device, mesh=mesh, in_specs=in_specs, out_specs=out_specs, check_vma=False
    )
```

```python
import math

import jax
import jax.numpy as jnp
from jax import lax
from jax.experimental import pallas as pl
from jax.experimental.pallas import tpu as pltpu
from jax.sharding import PartitionSpec as P

row_rate = 0.25
epsilon = 1e-06
unsent = 1e30
BF = jnp.bfloat16
F32 = jnp.float32
MESH = pl.DeviceIdType.MESH
NN = (((1,), (0,)), ((), ()))
NT = (((1,), (1,)), ((), ()))
TN = (((0,), (0,)), ((), ()))

SHARDS = 64
SLOTS = 8
BAGS = 4
N = 512
E = 128
H = 1024
HOT = 1024
COLD = 2048
TABLE = HOT + COLD
PIECE = H // SHARDS
BLK = 8
SPAN = 256
CHUNKS = ((0, 384), (384, 384), (768, 256))


def dot(lhs, rhs, dims=NN):
    return lax.dot_general(lhs, rhs, dims, preferred_element_type=F32)


def sigmoid(value):
    return 0.5 * jnp.tanh(0.5 * value) + 0.5


def step_rows(old_rows, grad_rows):
    scale_rows = jnp.sqrt(jnp.mean(grad_rows * grad_rows, axis=-1, keepdims=True) + epsilon)
    return old_rows.astype(F32) - row_rate * grad_rows / scale_rows


def part(index, size):
    return pl.ds(pl.multiple_of(index * size, size), size)


def identity():
    rows = lax.broadcasted_iota(jnp.int32, (E, E), 0)
    return (rows == lax.broadcasted_iota(jnp.int32, (E, E), 1)).astype(F32).astype(BF)


def first_row(value):
    return lax.broadcasted_iota(jnp.int32, (16, N), 0) == 0


def slot_rows(ids, slot):
    own = [ids[slot, bag][None, :] for bag in range(BAGS)]
    mult = [sum((one == other).astype(F32) for other in own).astype(BF) for one in own]
    return own, mult


def count_block(own, mult, block):
    spots = lax.broadcasted_iota(jnp.int32, (SPAN, N), 0).astype(F32).astype(BF)
    acc = jnp.zeros((SPAN, N), BF)
    for bag in range(BAGS):
        at = jnp.clip(own[bag] - block * SPAN, -1, SPAN).astype(F32).astype(BF)
        acc = jnp.where(spots == at, mult[bag], acc)
    return acc


def line_of(ref, axis, index, cols):
    at = [slice(None)] * 3
    at[axis] = index
    return ref.at[(*at, slice(None), cols)]


def shard_of(coords):
    return coords[0] * 16 + coords[1] * 4 + coords[2]


def on_line(coords, axis, index):
    return shard_of([index if other == axis else coords[other] for other in range(3)])


def in_plane(coords, axis, index):
    spots = iter((index // 4, lax.rem(index, 4)))
    return shard_of([coords[axis] if other == axis else next(spots) for other in range(3)])


def plane_index(coords, axis):
    first, second = [coords[other] for other in range(3) if other != axis]
    return first * 4 + second


def round_kernel(
    ids, labels, hot, cold, weight, bias_in, weight_out, owner, pushed,
    scores, cold_out, hot_after, weight_after,
    counts, table_t, pooled_t, pre_t, hidden_t, grad_t, grad_rows, pool_acc,
    gw, rw0, rw1, rw2, line0, line1, line2, plane0, plane1, plane2, allw, gh, rh, allh, piece_w, piece_h, learned, outgoing, arrived, small, wide,
    next_w, bias, wout, source_rows, source, sends, recvs, local,
):
    role = lax.axis_index("role")
    me = lax.axis_index("shard")
    coords = (me // 16, lax.rem(me // 4, 4), lax.rem(me, 4))
    rw, line, plane = (rw0, rw1, rw2), (line0, line1, line2), (plane0, plane1, plane2)
    barrier = pltpu.get_barrier_semaphore()
    top = lax.broadcasted_iota(jnp.int32, (16, H), 0) == 0
    bias[...] = jnp.where(top, bias_in[...].reshape(1, H).astype(F32), 0.0).astype(BF)
    wout[...] = jnp.where(top, weight_out[...].reshape(1, H).astype(F32), 0.0).astype(BF)

    def send_all(lo, source_of, target, sem_out, sem_in):
        def body(step, carry):
            to = lax.rem(me + step, SHARDS)
            pltpu.make_async_remote_copy(
                source_of(to), target, sem_out, sem_in, (1, to), MESH
            ).start()
            return carry

        lax.fori_loop(lo, SHARDS, body, 0)

    def drain(ref, sem):
        pltpu.make_async_copy(ref, ref, sem).wait()

    @pl.when(role == 1)
    def _():
        def greet(step, carry):
            pl.semaphore_signal(barrier, inc=1, device_id=(0, step), device_id_type=MESH)

            @pl.when(step != me)
            def _():
                pl.semaphore_signal(barrier, inc=1, device_id=(1, step), device_id_type=MESH)

            return carry

        lax.fori_loop(0, SHARDS, greet, 0)

    @pl.when(role == 0)
    def _():
        pl.semaphore_signal(barrier, inc=1, device_id=(1, me), device_id_type=MESH)
        groups = lax.broadcasted_iota(jnp.int32, (SHARDS, SHARDS), 1)
        owners = lax.broadcasted_iota(jnp.int32, (SHARDS, SHARDS), 0)
        found = jnp.where(owner[...] == owners, groups, 0)
        spot = jnp.clip(jnp.sum(found, axis=1, keepdims=True), 0, SHARDS - 1)
        source_rows[...] = jnp.broadcast_to(spot, (SHARDS, E))
        fetch = pltpu.make_async_copy(source_rows, source, local.at[0])
        fetch.start()
        eye = identity()
        table_t[:, :HOT] = dot(eye, hot[...], NT).astype(BF)
        table_t[:, HOT:] = dot(eye, cold[...], NT).astype(BF)

        def pool_slot(slot, carry):
            own, mult = slot_rows(ids, slot)
            lanes = part(slot, N)

            def build(block, carry):
                counts[part(block, SPAN), lanes] = count_block(own, mult, block)
                return carry

            lax.fori_loop(0, TABLE // SPAN, build, 0)
            pooled_t[part(slot, E), :] = dot(table_t[...], counts[:, lanes]).astype(BF)
            return carry

        lax.fori_loop(0, SLOTS, pool_slot, 0)
        first = lax.broadcasted_iota(jnp.int32, (16, N), 0) == 0
        ones = first.astype(F32).astype(BF)

        def forward(chunk, logit):
            cols = part(chunk, 256)
            pre = dot(weight[:, cols], pooled_t[...], TN) + dot(bias[:, cols], ones, TN)
            pre_t[cols, :] = pre
            hidden = (pre * sigmoid(pre)).astype(BF)
            hidden_t[cols, :] = hidden
            return logit + dot(wout[:, cols], hidden)

        logit = lax.fori_loop(0, H // 256, forward, jnp.zeros((16, N), F32))
        scores[...] = logit[0:1]
        slope = jnp.where(first, sigmoid(logit) - labels[...].reshape(1, N), 0.0).astype(BF)

        def backward(chunk, carry):
            cols = part(chunk, 256)
            pre = pre_t[cols, :]
            gate = sigmoid(pre)
            grad = (dot(wout[:, cols], slope, TN) * (gate * (1.0 + pre * (1.0 - gate)))).astype(BF)
            grad_t[cols, :] = grad
            wide[0:16, cols] = dot(ones, grad, NT)
            wide[16:32, cols] = dot(slope, hidden_t[cols, :], NT)
            return carry

        lax.fori_loop(0, H // 256, backward, 0)
        pl.semaphore_wait(barrier, SHARDS)

        for axis, (first_col, width) in enumerate(CHUNKS):
            cols = pl.ds(first_col, width)

            def dense(chunk, carry):
                rows = dot(pooled_t[part(chunk, 256), :], grad_t[cols, :], NT).astype(BF)
                gw[chunk, :, :, :, cols] = rows.reshape(4, 4, PIECE, width)
                return carry

            lax.fori_loop(0, 4, dense, 0)
            for step in range(4):
                index = lax.rem(coords[axis] + step, 4)
                pltpu.make_async_remote_copy(
                    line_of(gw, axis, index, cols),
                    rw[axis].at[coords[axis]],
                    sends.at[0],
                    recvs.at[axis],
                    (1, on_line(coords, axis, index)),
                    MESH,
                ).start()

        def rows_grad(slot, carry):
            grad_rows[:, part(slot, N)] = dot(weight[part(slot, E), :], grad_t[...]).astype(BF)
            return carry

        lax.fori_loop(0, SLOTS, rows_grad, 0)
        for row in range(8):
            small[row : row + 1, :] = wide[0:1, row * E : (row + 1) * E]
            small[row + 8 : row + 9, :] = wide[16:17, row * E : (row + 1) * E]
        small_piece = jnp.broadcast_to(small[...].astype(BF)[None], (16, PIECE, E))

        def hot_grad(block, carry):
            rows = dot(counts[part(block, SPAN), :], grad_rows[...], NT).astype(BF)
            gh[part(block, 16), 0:PIECE, :] = rows.reshape(16, PIECE, E)
            gh[part(block, 16), PIECE : 2 * PIECE, :] = small_piece
            return carry

        lax.fori_loop(0, HOT // SPAN, hot_grad, 0)
        send_all(0, lambda to: gh.at[to], rh.at[me], sends.at[1], recvs.at[12])

        def cold_grad(block, carry):
            grad = dot(counts[pl.ds(pl.multiple_of(HOT + block * SPAN, SPAN), SPAN), :], grad_rows[...], NT)
            rows = part(block, SPAN)
            fresh = step_rows(cold[rows, :], grad)
            cold_out[rows, :] = fresh.astype(BF)
            marked = [
                jnp.where(pushed[block * (SPAN // BLK) + at] == 1, fresh[at * BLK : (at + 1) * BLK], unsent)
                for at in range(SPAN // BLK)
            ]
            learned[part(block, 8)] = jnp.concatenate(marked, axis=0).astype(BF).reshape(8, 32, E)
            return carry

        lax.fori_loop(0, COLD // SPAN, cold_grad, 0)

        fetch.wait()

        def arrange(step, carry):
            outgoing[step] = learned[jnp.clip(source[step, 0], 0, SHARDS - 1)]
            return carry

        lax.fori_loop(0, SHARDS, arrange, 0)
        send_all(0, lambda to: outgoing.at[to], arrived.at[me], sends.at[2], recvs.at[13])
        drain(gw, sends.at[0])
        drain(gh, sends.at[1])
        drain(outgoing, sends.at[2])
        drain(weight_after, recvs.at[15])
        drain(hot_after, recvs.at[16])

    @pl.when(role == 1)
    def _():
        def count_slot(slot, carry):
            own, mult = slot_rows(ids, slot)
            lanes = part(slot, N)

            def build(block, carry):
                counts[part(block, SPAN), lanes] = count_block(own, mult, block)
                return carry

            return lax.fori_loop(0, TABLE // SPAN, build, carry)

        lax.fori_loop(0, SLOTS, count_slot, 0)
        pl.semaphore_wait(barrier, SHARDS)
        for axis, (first_col, width) in enumerate(CHUNKS):
            drain(rw[axis], recvs.at[axis])

            def add_line(step, carry):
                at = (step // 4, lax.rem(step, 4))
                total = sum(rw[axis][(source, *at)].astype(F32) for source in range(4))
                line[axis][step] = total.astype(BF)
                return carry

            lax.fori_loop(0, 16, add_line, 0)
            own = plane_index(coords, axis)

            def send_plane(step, carry):
                index = lax.rem(own + step, 16)
                pltpu.make_async_remote_copy(
                    line[axis].at[index],
                    plane[axis].at[own],
                    sends.at[axis],
                    recvs.at[3 + axis],
                    (1, in_plane(coords, axis, index)),
                    MESH,
                ).start()
                return carry

            lax.fori_loop(1, 16, send_plane, 0)
            plane[axis][own] = line[axis][own]
        for axis, (first_col, width) in enumerate(CHUNKS):
            cols = pl.ds(first_col, width)
            drain(plane[axis].at[pl.ds(0, 15)], recvs.at[3 + axis])
            total = lax.fori_loop(
                0,
                16,
                lambda step, total: total + plane[axis][step].astype(F32),
                jnp.zeros((PIECE, width), F32),
            ).astype(BF)
            piece_w[:, cols] = total
            allw[(*coords, slice(None), cols)] = total
            own = plane_index(coords, axis)

            def spread_plane(step, carry):
                pltpu.make_async_remote_copy(
                    piece_w.at[:, cols],
                    allw.at[(*coords, slice(None), cols)],
                    sends.at[3 + axis],
                    recvs.at[6 + axis],
                    (1, in_plane(coords, axis, lax.rem(own + step, 16))),
                    MESH,
                ).start()
                return carry

            lax.fori_loop(1, 16, spread_plane, 0)
        drain(rh, recvs.at[12])
        total = lax.fori_loop(
            0,
            SHARDS,
            lambda step, total: total + rh[step].astype(F32),
            jnp.zeros((2 * PIECE, E), F32),
        )
        piece_h[...] = step_rows(hot[part(me, PIECE), :], total[:PIECE]).astype(BF)
        send_all(1, lambda to: piece_h, allh.at[me], sends.at[9], recvs.at[14])
        allh[me] = piece_h[...]
        hot_after[...] = piece_h[...]
        for axis, (first_col, width) in enumerate(CHUNKS):
            cols = pl.ds(first_col, width)
            drain(plane[axis].at[pl.ds(0, 15)], recvs.at[6 + axis])
            for step in range(1, 4):
                index = lax.rem(coords[axis] + step, 4)
                pltpu.make_async_remote_copy(
                    line_of(allw, axis, coords[axis], cols),
                    line_of(allw, axis, coords[axis], cols),
                    sends.at[6 + axis],
                    recvs.at[9 + axis],
                    (1, on_line(coords, axis, index)),
                    MESH,
                ).start()
        sums = total[PIECE:]
        bias_sum, out_sum = sums[:8], sums[8:]
        bias_scale = 0.5 / jnp.sqrt(jnp.mean(bias_sum * bias_sum, keepdims=True) + epsilon)
        out_scale = (1.0 / math.sqrt(H)) / jnp.sqrt(jnp.mean(out_sum * out_sum, keepdims=True) + epsilon)
        small[0:8, :] = bias_sum * bias_scale
        small[8:16, :] = out_sum * out_scale
        wide[...] = jnp.zeros(wide.shape, F32)
        for row in range(8):
            wide[0:1, row * E : (row + 1) * E] = small[row : row + 1, :]
            wide[16:17, row * E : (row + 1) * E] = small[row + 8 : row + 9, :]
        bias_next = (bias[...].astype(F32) - wide[0:16, :]).astype(BF)
        out_next = (wout[...].astype(F32) - wide[16:32, :]).astype(BF)
        small16 = bias_next, out_next
        wide[0:16, :] = small16[0].astype(F32)
        wide[16:32, :] = small16[1].astype(F32)

        drain(arrived, recvs.at[13])
        eye = identity()

        def merge(block, carry):
            rows = part(block, SPAN)
            came = arrived[part(block, 8)].reshape(SPAN, E)
            fresh = jnp.where(came < unsent * 0.5, came, cold[rows, :])
            cold_out[rows, :] = fresh
            table_t[:, pl.ds(pl.multiple_of(HOT + block * SPAN, SPAN), SPAN)] = dot(eye, fresh, NT).astype(BF)
            return carry

        lax.fori_loop(0, COLD // SPAN, merge, 0)

        def pool_cold(slot, carry):
            pool_acc[part(slot, E), :] = dot(table_t[:, HOT:], counts[HOT:, part(slot, N)])
            return carry

        lax.fori_loop(0, SLOTS, pool_cold, 0)
        drain(allh.at[pl.ds(0, SHARDS - 1)], recvs.at[14])
        table_t[:, :HOT] = dot(eye, allh[...].reshape(HOT, E), NT).astype(BF)

        def pool_hot(slot, carry):
            rows = part(slot, E)
            pooled_t[rows, :] = (
                pool_acc[rows, :] + dot(table_t[:, :HOT], counts[:HOT, part(slot, N)])
            ).astype(BF)
            return carry

        lax.fori_loop(0, SLOTS, pool_hot, 0)
        for axis in range(3):
            drain(rw[axis].at[pl.ds(0, 3)], recvs.at[9 + axis])

        def squares(step, total):
            value = allw[step // 16, lax.rem(step // 4, 4), lax.rem(step, 4)].astype(F32)
            return total + value * value

        total = lax.fori_loop(0, SHARDS, squares, jnp.zeros((PIECE, H), F32))
        scale = (1.0 / math.sqrt(H)) / jnp.sqrt(jnp.sum(total, keepdims=True) / (H * H) + epsilon)

        def update(step, carry):
            rows = part(step, PIECE)
            next_w[rows, :] = (
                weight[rows, :].astype(F32) - allw[step // 16, lax.rem(step // 4, 4), lax.rem(step, 4)].astype(F32) * scale
            ).astype(BF)
            return carry

        lax.fori_loop(0, SHARDS, update, 0)
        weight_after[...] = next_w[part(me, PIECE), :]
        piece_w2 = next_w.at[part(me, PIECE)]
        for axis in range(3):
            drain(plane[axis].at[pl.ds(0, 15)], sends.at[axis])
            drain(plane[axis].at[pl.ds(0, 15)], sends.at[3 + axis])
            drain(rw[axis].at[pl.ds(0, 3)], sends.at[6 + axis])
        drain(allh.at[pl.ds(0, SHARDS - 1)], sends.at[9])
        final_w = pltpu.make_async_remote_copy(
            piece_w2, weight_after, sends.at[10], recvs.at[15], (0, me), MESH
        )
        final_h = pltpu.make_async_remote_copy(
            piece_h, hot_after, sends.at[11], recvs.at[16], (0, me), MESH
        )
        final_w.start()
        final_h.start()
        ones = (lax.broadcasted_iota(jnp.int32, (16, N), 0) == 0).astype(F32).astype(BF)

        def score(chunk, logit):
            cols = part(chunk, 256)
            pre = dot(next_w[:, cols], pooled_t[...], TN) + dot(wide[0:16, cols].astype(BF), ones, TN)
            hidden = (pre * sigmoid(pre)).astype(BF)
            return logit + dot(wide[16:32, cols].astype(BF), hidden)

        scores[...] = lax.fori_loop(0, H // 256, score, jnp.zeros((16, N), F32))[0:1]
        final_w.wait_send()
        final_h.wait_send()


def run_round(ids, labels, hot, cold, weight, bias, wout, owner, pushed):
    vmem = pl.BlockSpec(memory_space=pltpu.VMEM)
    smem = pl.BlockSpec(memory_space=pltpu.SMEM)
    return pl.pallas_call(
        round_kernel,
        out_shape=(
            jax.ShapeDtypeStruct((1, N), F32),
            jax.ShapeDtypeStruct((COLD, E), BF),
            jax.ShapeDtypeStruct((PIECE, E), BF),
            jax.ShapeDtypeStruct((PIECE, H), BF),
        ),
        in_specs=[vmem] * 8 + [smem],
        out_specs=(vmem,) * 4,
        scratch_shapes=[
            pltpu.VMEM((TABLE, SLOTS * N), BF),
            pltpu.VMEM((E, TABLE), BF),
            pltpu.VMEM((H, N), BF),
            pltpu.VMEM((H, N), F32),
            pltpu.VMEM((H, N), BF),
            pltpu.VMEM((H, N), BF),
            pltpu.VMEM((E, SLOTS * N), BF),
            pltpu.VMEM((H, N), F32),
            pltpu.VMEM((4, 4, 4, PIECE, H), BF),
            *[pltpu.VMEM((4, 4, 4, PIECE, width), BF) for _, width in CHUNKS],
            *[pltpu.VMEM((16, PIECE, width), BF) for _, width in CHUNKS],
            *[pltpu.VMEM((16, PIECE, width), BF) for _, width in CHUNKS],
            pltpu.VMEM((4, 4, 4, PIECE, H), BF),
            pltpu.VMEM((SHARDS, 2 * PIECE, E), BF),
            pltpu.VMEM((SHARDS, 2 * PIECE, E), BF),
            pltpu.VMEM((SHARDS, PIECE, E), BF),
            pltpu.VMEM((PIECE, H), BF),
            pltpu.VMEM((PIECE, E), BF),
            pltpu.VMEM((SHARDS, 32, E), BF),
            pltpu.VMEM((SHARDS, 32, E), BF),
            pltpu.VMEM((SHARDS, 32, E), BF),
            pltpu.VMEM((16, E), F32),
            pltpu.VMEM((32, H), F32),
            pltpu.VMEM((H, H), BF),
            pltpu.VMEM((16, H), BF),
            pltpu.VMEM((16, H), BF),
            pltpu.VMEM((SHARDS, E), jnp.int32),
            pltpu.SMEM((SHARDS, E), jnp.int32),
            pltpu.SemaphoreType.DMA((12,)),
            pltpu.SemaphoreType.DMA((17,)),
            pltpu.SemaphoreType.DMA((1,)),
        ],
        compiler_params=pltpu.CompilerParams(
            collective_id=0, has_side_effects=True, vmem_limit_bytes=58 << 20
        ),
        name="round",
    )(ids, labels, hot, cold, weight, bias, wout, owner, pushed)


def hand_over_kernel(*refs):
    count = len(refs) // 2
    copies = [
        pltpu.make_async_copy(refs[at], refs[count + at], refs[-1].at[at]) for at in range(count)
    ]
    for copy in copies:
        copy.start()
    for copy in copies:
        copy.wait()


def hand_over(arrays):
    return pl.pallas_call(
        hand_over_kernel,
        out_shape=tuple(jax.ShapeDtypeStruct(array.shape, array.dtype) for array in arrays),
        in_specs=[pl.BlockSpec(memory_space=pl.ANY)] * len(arrays),
        out_specs=(pl.BlockSpec(memory_space=pltpu.VMEM),) * len(arrays),
        scratch_shapes=[pltpu.SemaphoreType.DMA((len(arrays),))],
        name="hand_over",
    )(*arrays)


def on_device(
    feature_ids, labels, cold_rows, hot_rows, block_owner, pushed, weight_in, bias_in, weight_out
):
    scores, cold_out, hot_after, weight_after = hand_over(
        run_round(
            feature_ids[0],
            labels,
            hot_rows,
            cold_rows[0],
            weight_in,
            bias_in,
            weight_out,
            block_owner,
            pushed,
        )
    )
    return (scores, cold_out[None], hot_after, weight_after)


def solution(mesh):
    in_specs = (
        P("role", None, None, "shard"),
        P("shard"),
        P("role", "shard", None),
        P(),
        P("shard", None),
        P("shard"),
        P(),
        P(),
        P(),
    )
    out_specs = (P("role", "shard"), P("role", "shard", None), P("shard", None), P("shard", None))
    return jax.shard_map(
        on_device, mesh=mesh, in_specs=in_specs, out_specs=out_specs, check_vma=False
    )
```

```python
import math

import jax
import jax.numpy as jnp
from jax import lax
from jax.experimental import pallas as pl
from jax.experimental.pallas import tpu as pltpu
from jax.sharding import PartitionSpec as P

row_rate = 0.25
epsilon = 1e-06
unsent = 1e30
BF = jnp.bfloat16
F32 = jnp.float32
MESH = pl.DeviceIdType.MESH
NN = (((1,), (0,)), ((), ()))
NT = (((1,), (1,)), ((), ()))
TN = (((0,), (0,)), ((), ()))

SHARDS = 64
SLOTS = 8
BAGS = 4
N = 512
E = 128
H = 1024
HOT = 1024
COLD = 2048
TABLE = HOT + COLD
PIECE = H // SHARDS
BLK = 8
SPAN = 256
STEP = 512
CHUNKS = ((0, 384), (384, 384), (768, 256))


def dot(lhs, rhs, dims=NN):
    return lax.dot_general(lhs, rhs, dims, preferred_element_type=F32)


def sigmoid(value):
    return 0.5 * jnp.tanh(0.5 * value) + 0.5


def step_rows(old_rows, grad_rows):
    scale_rows = row_rate * lax.rsqrt(jnp.mean(grad_rows * grad_rows, axis=-1, keepdims=True) + epsilon)
    return old_rows.astype(F32) - grad_rows * scale_rows


def part(index, size):
    return pl.ds(pl.multiple_of(index * size, size), size)


def identity():
    rows = lax.broadcasted_iota(jnp.int32, (E, E), 0)
    return (rows == lax.broadcasted_iota(jnp.int32, (E, E), 1)).astype(F32).astype(BF)


def first_row(value):
    return lax.broadcasted_iota(jnp.int32, (16, N), 0) == 0


def slot_rows(ids, slot):
    own = [ids[slot, bag][None, :] for bag in range(BAGS)]
    mult = [sum((one == other).astype(F32) for other in own).astype(BF) for one in own]
    return own, mult


def count_block(own, mult, block):
    spots = lax.broadcasted_iota(jnp.int32, (SPAN, N), 0).astype(F32).astype(BF)
    acc = jnp.zeros((SPAN, N), BF)
    for bag in range(BAGS):
        at = jnp.clip(own[bag] - block * SPAN, -1, SPAN).astype(F32).astype(BF)
        acc = jnp.where(spots == at, mult[bag], acc)
    return acc


def line_of(ref, axis, index, cols):
    at = [slice(None)] * 3
    at[axis] = index
    return ref.at[(*at, slice(None), cols)]


def shard_of(coords):
    return coords[0] * 16 + coords[1] * 4 + coords[2]


def on_line(coords, axis, index):
    return shard_of([index if other == axis else coords[other] for other in range(3)])


def in_plane(coords, axis, index):
    spots = iter((index // 4, lax.rem(index, 4)))
    return shard_of([coords[axis] if other == axis else next(spots) for other in range(3)])


def plane_index(coords, axis):
    first, second = [coords[other] for other in range(3) if other != axis]
    return first * 4 + second


def round_kernel(
    ids, labels, hot, cold, weight, bias_in, weight_out, owner, pushed,
    scores, cold_out, hot_after, weight_after,
    counts, table_t, pooled_t, pre_t, hidden_t, grad_t, grad_rows, pool_acc,
    gw, rw0, rw1, rw2, line0, line1, line2, plane0, plane1, plane2, allw, gh, rh, allh, piece_w, piece_h, learned, outgoing, arrived, small, wide,
    bias, wout, source_rows, source, sends, recvs, local,
):
    role = lax.axis_index("role")
    me = lax.axis_index("shard")
    coords = (me // 16, lax.rem(me // 4, 4), lax.rem(me, 4))
    rw, line, plane = (rw0, rw1, rw2), (line0, line1, line2), (plane0, plane1, plane2)
    barrier = pltpu.get_barrier_semaphore()
    top = lax.broadcasted_iota(jnp.int32, (16, H), 0) == 0
    bias[...] = jnp.where(top, bias_in[...].reshape(1, H).astype(F32), 0.0).astype(BF)
    wout[...] = jnp.where(top, weight_out[...].reshape(1, H).astype(F32), 0.0).astype(BF)

    def send_all(lo, source_of, target, sem_out, sem_in):
        def body(step, carry):
            to = lax.rem(me + step, SHARDS)
            pltpu.make_async_remote_copy(
                source_of(to), target, sem_out, sem_in, (1, to), MESH
            ).start()
            return carry

        lax.fori_loop(lo, SHARDS, body, 0)

    def drain(ref, sem):
        pltpu.make_async_copy(ref, ref, sem).wait()

    @pl.when(role == 1)
    def _():
        def greet(step, carry):
            pl.semaphore_signal(barrier, inc=1, device_id=(0, step), device_id_type=MESH)

            @pl.when(step != me)
            def _():
                pl.semaphore_signal(barrier, inc=1, device_id=(1, step), device_id_type=MESH)

            return carry

        lax.fori_loop(0, SHARDS, greet, 0)

    @pl.when(role == 0)
    def _():
        pl.semaphore_signal(barrier, inc=1, device_id=(1, me), device_id_type=MESH)
        groups = lax.broadcasted_iota(jnp.int32, (SHARDS, SHARDS), 1)
        owners = lax.broadcasted_iota(jnp.int32, (SHARDS, SHARDS), 0)
        found = jnp.where(owner[...] == owners, groups, 0)
        spot = jnp.clip(jnp.sum(found, axis=1, keepdims=True), 0, SHARDS - 1)
        source_rows[...] = jnp.broadcast_to(spot, (SHARDS, E))
        fetch = pltpu.make_async_copy(source_rows, source, local.at[0])
        fetch.start()
        eye = identity()
        table_t[:, :HOT] = dot(eye, hot[...], NT).astype(BF)
        table_t[:, HOT:] = dot(eye, cold[...], NT).astype(BF)

        for slot in range(SLOTS):
            own, mult = slot_rows(ids, slot)
            lanes = slice(slot * N, (slot + 1) * N)
            for block in range(TABLE // SPAN):
                counts[block * SPAN : (block + 1) * SPAN, lanes] = count_block(own, mult, block)
            pooled_t[slot * E : (slot + 1) * E, :] = dot(table_t[...], counts[:, lanes]).astype(BF)
        first = lax.broadcasted_iota(jnp.int32, (16, N), 0) == 0
        ones = first.astype(F32).astype(BF)

        def forward(chunk, logit):
            cols = part(chunk, 256)
            pre = dot(weight[:, cols], pooled_t[...], TN) + dot(bias[:, cols], ones, TN)
            pre_t[cols, :] = pre
            hidden = (pre * sigmoid(pre)).astype(BF)
            hidden_t[cols, :] = hidden
            return logit + dot(wout[:, cols], hidden)

        logit = lax.fori_loop(0, H // 256, forward, jnp.zeros((16, N), F32))
        scores[...] = logit[0:1]
        slope = jnp.where(first, sigmoid(logit) - labels[...].reshape(1, N), 0.0).astype(BF)

        def backward(chunk, carry):
            cols = part(chunk, 256)
            pre = pre_t[cols, :]
            gate = sigmoid(pre)
            grad = (dot(wout[:, cols], slope, TN) * (gate * (1.0 + pre * (1.0 - gate)))).astype(BF)
            grad_t[cols, :] = grad
            wide[0:16, cols] = dot(ones, grad, NT)
            wide[16:32, cols] = dot(slope, hidden_t[cols, :], NT)
            return carry

        lax.fori_loop(0, H // 256, backward, 0)
        pl.semaphore_wait(barrier, SHARDS)

        for axis, (first_col, width) in enumerate(CHUNKS):
            cols = pl.ds(first_col, width)

            def dense(chunk, carry):
                rows = dot(pooled_t[part(chunk, 256), :], grad_t[cols, :], NT).astype(BF)
                gw[chunk, :, :, :, cols] = rows.reshape(4, 4, PIECE, width)
                return carry

            lax.fori_loop(0, 4, dense, 0)
            for step in range(4):
                index = lax.rem(coords[axis] + step, 4)
                pltpu.make_async_remote_copy(
                    line_of(gw, axis, index, cols),
                    rw[axis].at[coords[axis]],
                    sends.at[0],
                    recvs.at[axis],
                    (1, on_line(coords, axis, index)),
                    MESH,
                ).start()

        def rows_grad(slot, carry):
            grad_rows[:, part(slot, N)] = dot(weight[part(slot, E), :], grad_t[...]).astype(BF)
            return carry

        lax.fori_loop(0, SLOTS, rows_grad, 0)
        for row in range(8):
            small[row : row + 1, :] = wide[0:1, row * E : (row + 1) * E]
            small[row + 8 : row + 9, :] = wide[16:17, row * E : (row + 1) * E]
        small_piece = jnp.broadcast_to(small[...].astype(BF)[None], (16, PIECE, E))

        for block in range(HOT // STEP):
            rows = dot(counts[block * STEP : (block + 1) * STEP, :], grad_rows[...], NT).astype(BF)
            at = pl.ds(block * (STEP // PIECE), STEP // PIECE)
            gh[at, 0:PIECE, :] = rows.reshape(STEP // PIECE, PIECE, E)
        for block in range(4):
            gh[block * 16 : block * 16 + 16, PIECE : 2 * PIECE, :] = small_piece
        send_all(0, lambda to: gh.at[to], rh.at[me], sends.at[1], recvs.at[12])
        for block in range(COLD // STEP):
            rows = pl.ds(block * STEP, STEP)
            grad = dot(counts[pl.ds(HOT + block * STEP, STEP), :], grad_rows[...], NT)
            fresh = step_rows(cold[rows, :], grad)
            cold_out[rows, :] = fresh.astype(BF)
            marked = [
                jnp.where(
                    pushed[block * (STEP // BLK) + at] == 1, fresh[at * BLK : (at + 1) * BLK], unsent
                )
                for at in range(STEP // BLK)
            ]
            groups_here = pl.ds(block * (STEP // 32), STEP // 32)
            learned[groups_here] = jnp.concatenate(marked, axis=0).astype(BF).reshape(-1, 32, E)
        fetch.wait()

        def arrange(step, carry):
            outgoing[step] = learned[jnp.clip(source[step, 0], 0, SHARDS - 1)]
            return carry

        lax.fori_loop(0, SHARDS, arrange, 0)
        send_all(0, lambda to: outgoing.at[to], arrived.at[me], sends.at[2], recvs.at[13])
        drain(gw, sends.at[0])
        drain(gh, sends.at[1])
        drain(outgoing, sends.at[2])
        drain(weight_after, recvs.at[15])
        drain(hot_after, recvs.at[16])

    @pl.when(role == 1)
    def _():
        def count_slot(slot, carry):
            own, mult = slot_rows(ids, slot)
            lanes = part(slot, N)

            def build(block, carry):
                counts[part(block, SPAN), lanes] = count_block(own, mult, block)
                return carry

            return lax.fori_loop(0, TABLE // SPAN, build, carry)

        lax.fori_loop(0, SLOTS, count_slot, 0)
        pl.semaphore_wait(barrier, SHARDS)
        for axis, (first_col, width) in enumerate(CHUNKS):
            drain(rw[axis], recvs.at[axis])

            def add_line(step, carry):
                at = (step // 4, lax.rem(step, 4))
                total = sum(rw[axis][(source, *at)].astype(F32) for source in range(4))
                line[axis][step] = total.astype(BF)
                return carry

            lax.fori_loop(0, 16, add_line, 0)
            own = plane_index(coords, axis)

            def send_plane(step, carry):
                index = lax.rem(own + step, 16)
                pltpu.make_async_remote_copy(
                    line[axis].at[index],
                    plane[axis].at[own],
                    sends.at[axis],
                    recvs.at[3 + axis],
                    (1, in_plane(coords, axis, index)),
                    MESH,
                ).start()
                return carry

            lax.fori_loop(1, 16, send_plane, 0)
            plane[axis][own] = line[axis][own]
        for axis, (first_col, width) in enumerate(CHUNKS):
            cols = pl.ds(first_col, width)
            drain(plane[axis].at[pl.ds(0, 15)], recvs.at[3 + axis])
            total = lax.fori_loop(
                0,
                16,
                lambda step, total: total + plane[axis][step].astype(F32),
                jnp.zeros((PIECE, width), F32),
            ).astype(BF)
            piece_w[:, cols] = total
            allw[(*coords, slice(None), cols)] = total
            own = plane_index(coords, axis)

            def spread_plane(step, carry):
                pltpu.make_async_remote_copy(
                    piece_w.at[:, cols],
                    allw.at[(*coords, slice(None), cols)],
                    sends.at[3 + axis],
                    recvs.at[6 + axis],
                    (1, in_plane(coords, axis, lax.rem(own + step, 16))),
                    MESH,
                ).start()
                return carry

            lax.fori_loop(1, 16, spread_plane, 0)
        drain(rh, recvs.at[12])
        total = lax.fori_loop(
            0,
            SHARDS,
            lambda step, total: total + rh[step].astype(F32),
            jnp.zeros((2 * PIECE, E), F32),
        )
        piece_h[...] = step_rows(hot[part(me, PIECE), :], total[:PIECE]).astype(BF)
        send_all(1, lambda to: piece_h, allh.at[me], sends.at[9], recvs.at[14])
        allh[me] = piece_h[...]
        hot_after[...] = piece_h[...]
        for axis, (first_col, width) in enumerate(CHUNKS):
            cols = pl.ds(first_col, width)
            drain(plane[axis].at[pl.ds(0, 15)], recvs.at[6 + axis])
            for step in range(1, 4):
                index = lax.rem(coords[axis] + step, 4)
                pltpu.make_async_remote_copy(
                    line_of(allw, axis, coords[axis], cols),
                    line_of(allw, axis, coords[axis], cols),
                    sends.at[6 + axis],
                    recvs.at[9 + axis],
                    (1, on_line(coords, axis, index)),
                    MESH,
                ).start()
        sums = total[PIECE:]
        bias_sum, out_sum = sums[:8], sums[8:]
        bias_scale = 0.5 / jnp.sqrt(jnp.mean(bias_sum * bias_sum, keepdims=True) + epsilon)
        out_scale = (1.0 / math.sqrt(H)) / jnp.sqrt(jnp.mean(out_sum * out_sum, keepdims=True) + epsilon)
        small[0:8, :] = bias_sum * bias_scale
        small[8:16, :] = out_sum * out_scale
        wide[...] = jnp.zeros(wide.shape, F32)
        for row in range(8):
            wide[0:1, row * E : (row + 1) * E] = small[row : row + 1, :]
            wide[16:17, row * E : (row + 1) * E] = small[row + 8 : row + 9, :]
        bias_next = (bias[...].astype(F32) - wide[0:16, :]).astype(BF)
        out_next = (wout[...].astype(F32) - wide[16:32, :]).astype(BF)
        small16 = bias_next, out_next
        wide[0:16, :] = small16[0].astype(F32)
        wide[16:32, :] = small16[1].astype(F32)

        drain(allh.at[pl.ds(0, SHARDS - 1)], recvs.at[14])
        eye = identity()
        table_t[:, :HOT] = dot(eye, allh[...].reshape(HOT, E), NT).astype(BF)

        def pool_hot(slot, carry):
            pool_acc[part(slot, E), :] = dot(table_t[:, :HOT], counts[:HOT, part(slot, N)])
            return carry

        lax.fori_loop(0, SLOTS, pool_hot, 0)
        drain(arrived, recvs.at[13])

        def merge(block, carry):
            rows = part(block, SPAN)
            came = arrived[part(block, 8)].reshape(SPAN, E)
            fresh = jnp.where(came < unsent * 0.5, came, cold[rows, :])
            cold_out[rows, :] = fresh
            table_t[:, pl.ds(pl.multiple_of(HOT + block * SPAN, SPAN), SPAN)] = dot(eye, fresh, NT).astype(BF)
            return carry

        lax.fori_loop(0, COLD // SPAN, merge, 0)

        def pool_cold(slot, carry):
            rows = part(slot, E)
            pooled_t[rows, :] = (
                pool_acc[rows, :] + dot(table_t[:, HOT:], counts[HOT:, part(slot, N)])
            ).astype(BF)
            return carry

        lax.fori_loop(0, SLOTS, pool_cold, 0)
        ones = (lax.broadcasted_iota(jnp.int32, (16, N), 0) == 0).astype(F32).astype(BF)

        def before(chunk, carry):
            cols = part(chunk, 256)
            pre_t[cols, :] = dot(weight[:, cols], pooled_t[...], TN) + dot(
                wide[0:16, cols].astype(BF), ones, TN
            )
            return carry

        lax.fori_loop(0, H // 256, before, 0)
        for axis in range(3):
            drain(rw[axis].at[pl.ds(0, 3)], recvs.at[9 + axis])

        for axis in range(3):
            drain(plane[axis].at[pl.ds(0, 15)], sends.at[axis])
            drain(plane[axis].at[pl.ds(0, 15)], sends.at[3 + axis])
            drain(rw[axis].at[pl.ds(0, 3)], sends.at[6 + axis])
        drain(allh.at[pl.ds(0, SHARDS - 1)], sends.at[9])

        def squares(step, total):
            value = allw[step // 16, lax.rem(step // 4, 4), lax.rem(step, 4)].astype(F32)
            return total + value * value

        total = lax.fori_loop(0, SHARDS, squares, jnp.zeros((PIECE, H), F32))
        scale = (1.0 / math.sqrt(H)) / jnp.sqrt(jnp.sum(total, keepdims=True) / (H * H) + epsilon)

        weight_after[...] = (
            weight[part(me, PIECE), :].astype(F32) - allw[coords].astype(F32) * scale
        ).astype(BF)
        piece_w[...] = weight_after[...]
        final_w = pltpu.make_async_remote_copy(
            piece_w, weight_after, sends.at[10], recvs.at[15], (0, me), MESH
        )
        final_h = pltpu.make_async_remote_copy(
            piece_h, hot_after, sends.at[11], recvs.at[16], (0, me), MESH
        )
        final_w.start()
        final_h.start()

        def score(chunk, logit):
            cols = part(chunk, 256)
            grad = allw[:, :, :, :, cols].reshape(H, 256)
            pre = pre_t[cols, :] - dot(grad, pooled_t[...], TN) * scale
            hidden = (pre * sigmoid(pre)).astype(BF)
            return logit + dot(wide[16:32, cols].astype(BF), hidden)

        scores[...] = lax.fori_loop(0, H // 256, score, jnp.zeros((16, N), F32))[0:1]
        final_w.wait_send()
        final_h.wait_send()


def run_round(ids, labels, hot, cold, weight, bias, wout, owner, pushed):
    vmem = pl.BlockSpec(memory_space=pltpu.VMEM)
    smem = pl.BlockSpec(memory_space=pltpu.SMEM)
    return pl.pallas_call(
        round_kernel,
        out_shape=(
            jax.ShapeDtypeStruct((1, N), F32),
            jax.ShapeDtypeStruct((COLD, E), BF),
            jax.ShapeDtypeStruct((PIECE, E), BF),
            jax.ShapeDtypeStruct((PIECE, H), BF),
        ),
        in_specs=[vmem] * 8 + [smem],
        out_specs=(vmem,) * 4,
        scratch_shapes=[
            pltpu.VMEM((TABLE, SLOTS * N), BF),
            pltpu.VMEM((E, TABLE), BF),
            pltpu.VMEM((H, N), BF),
            pltpu.VMEM((H, N), F32),
            pltpu.VMEM((H, N), BF),
            pltpu.VMEM((H, N), BF),
            pltpu.VMEM((E, SLOTS * N), BF),
            pltpu.VMEM((H, N), F32),
            pltpu.VMEM((4, 4, 4, PIECE, H), BF),
            *[pltpu.VMEM((4, 4, 4, PIECE, width), BF) for _, width in CHUNKS],
            *[pltpu.VMEM((16, PIECE, width), BF) for _, width in CHUNKS],
            *[pltpu.VMEM((16, PIECE, width), BF) for _, width in CHUNKS],
            pltpu.VMEM((4, 4, 4, PIECE, H), BF),
            pltpu.VMEM((SHARDS, 2 * PIECE, E), BF),
            pltpu.VMEM((SHARDS, 2 * PIECE, E), BF),
            pltpu.VMEM((SHARDS, PIECE, E), BF),
            pltpu.VMEM((PIECE, H), BF),
            pltpu.VMEM((PIECE, E), BF),
            pltpu.VMEM((SHARDS, 32, E), BF),
            pltpu.VMEM((SHARDS, 32, E), BF),
            pltpu.VMEM((SHARDS, 32, E), BF),
            pltpu.VMEM((16, E), F32),
            pltpu.VMEM((32, H), F32),
            pltpu.VMEM((16, H), BF),
            pltpu.VMEM((16, H), BF),
            pltpu.VMEM((SHARDS, E), jnp.int32),
            pltpu.SMEM((SHARDS, E), jnp.int32),
            pltpu.SemaphoreType.DMA((12,)),
            pltpu.SemaphoreType.DMA((17,)),
            pltpu.SemaphoreType.DMA((1,)),
        ],
        compiler_params=pltpu.CompilerParams(
            collective_id=0, has_side_effects=True, vmem_limit_bytes=58 << 20
        ),
        name="round",
    )(ids, labels, hot, cold, weight, bias, wout, owner, pushed)


def hand_over_kernel(*refs):
    count = len(refs) // 2
    copies = [
        pltpu.make_async_copy(refs[at], refs[count + at], refs[-1].at[at]) for at in range(count)
    ]
    for copy in copies:
        copy.start()
    for copy in copies:
        copy.wait()


def hand_over(arrays):
    return pl.pallas_call(
        hand_over_kernel,
        out_shape=tuple(jax.ShapeDtypeStruct(array.shape, array.dtype) for array in arrays),
        in_specs=[pl.BlockSpec(memory_space=pl.ANY)] * len(arrays),
        out_specs=(pl.BlockSpec(memory_space=pltpu.VMEM),) * len(arrays),
        scratch_shapes=[pltpu.SemaphoreType.DMA((len(arrays),))],
        name="hand_over",
    )(*arrays)


def on_device(
    feature_ids, labels, cold_rows, hot_rows, block_owner, pushed, weight_in, bias_in, weight_out
):
    scores, cold_out, hot_after, weight_after = hand_over(
        run_round(
            feature_ids[0],
            labels,
            hot_rows,
            cold_rows[0],
            weight_in,
            bias_in,
            weight_out,
            block_owner,
            pushed,
        )
    )
    return (scores, cold_out[None], hot_after, weight_after)


def solution(mesh):
    in_specs = (
        P("role", None, None, "shard"),
        P("shard"),
        P("role", "shard", None),
        P(),
        P("shard", None),
        P("shard"),
        P(),
        P(),
        P(),
    )
    out_specs = (P("role", "shard"), P("role", "shard", None), P("shard", None), P("shard", None))
    return jax.shard_map(
        on_device, mesh=mesh, in_specs=in_specs, out_specs=out_specs, check_vma=False
    )
```

```python
import math

import jax
import jax.numpy as jnp
from jax import lax
from jax.experimental import pallas as pl
from jax.experimental.pallas import tpu as pltpu
from jax.sharding import PartitionSpec as P

row_rate = 0.25
epsilon = 1e-06
unsent = 1e30
BF = jnp.bfloat16
F32 = jnp.float32
MESH = pl.DeviceIdType.MESH
NN = (((1,), (0,)), ((), ()))
NT = (((1,), (1,)), ((), ()))
TN = (((0,), (0,)), ((), ()))

SHARDS = 64
SLOTS = 8
BAGS = 4
N = 512
E = 128
H = 1024
HOT = 1024
COLD = 2048
TABLE = HOT + COLD
PIECE = H // SHARDS
BLK = 8
SPAN = 256
STEP = 512
CHUNKS = ((0, 0, 384), (1, 384, 384), (2, 768, 256), (1, 0, 128))


def dot(lhs, rhs, dims=NN):
    return lax.dot_general(lhs, rhs, dims, preferred_element_type=F32)


def sigmoid(value):
    return 0.5 * jnp.tanh(0.5 * value) + 0.5


def step_rows(old_rows, grad_rows):
    scale_rows = row_rate * lax.rsqrt(jnp.mean(grad_rows * grad_rows, axis=-1, keepdims=True) + epsilon)
    return old_rows.astype(F32) - grad_rows * scale_rows


def part(index, size):
    return pl.ds(pl.multiple_of(index * size, size), size)


def identity():
    rows = lax.broadcasted_iota(jnp.int32, (E, E), 0)
    return (rows == lax.broadcasted_iota(jnp.int32, (E, E), 1)).astype(F32).astype(BF)


def first_row(value):
    return lax.broadcasted_iota(jnp.int32, (16, N), 0) == 0


def slot_rows(ids, slot):
    own = [ids[slot, bag][None, :] for bag in range(BAGS)]
    mult = [sum((one == other).astype(F32) for other in own).astype(BF) for one in own]
    return own, mult


def count_block(own, mult, block):
    spots = lax.broadcasted_iota(jnp.int32, (SPAN, N), 0).astype(F32).astype(BF)
    acc = jnp.zeros((SPAN, N), BF)
    for bag in range(BAGS):
        at = jnp.clip(own[bag] - block * SPAN, -1, SPAN).astype(F32).astype(BF)
        acc = jnp.where(spots == at, mult[bag], acc)
    return acc


def line_of(ref, axis, index, cols):
    at = [slice(None)] * 3
    at[axis] = index
    return ref.at[(*at, slice(None), cols)]


def shard_of(coords):
    return coords[0] * 16 + coords[1] * 4 + coords[2]


def on_line(coords, axis, index):
    return shard_of([index if other == axis else coords[other] for other in range(3)])


def in_plane(coords, axis, index):
    spots = iter((index // 4, lax.rem(index, 4)))
    return shard_of([coords[axis] if other == axis else next(spots) for other in range(3)])


def plane_index(coords, axis):
    first, second = [coords[other] for other in range(3) if other != axis]
    return first * 4 + second


def round_kernel(
    ids, labels, hot, cold, weight, bias_in, weight_out, owner, pushed,
    scores, cold_out, hot_after, weight_after,
    counts, table_t, pooled_t, pre_t, hidden_t, grad_t, grad_rows, pool_acc,
    gw, rw0, rw1, rw2, rw3, line0, line1, line2, line3, plane0, plane1, plane2, plane3, allw, gh, gs, rs, allh, piece_w, piece_h, learned, outgoing, arrived, small, wide,
    bias, wout, source_rows, source, sends, recvs, local,
):
    role = lax.axis_index("role")
    me = lax.axis_index("shard")
    coords = (me // 16, lax.rem(me // 4, 4), lax.rem(me, 4))
    rw, line = (rw0, rw1, rw2, rw3), (line0, line1, line2, line3)
    plane = (plane0, plane1, plane2, plane3)
    barrier = pltpu.get_barrier_semaphore()
    top = lax.broadcasted_iota(jnp.int32, (16, H), 0) == 0
    bias[...] = jnp.where(top, bias_in[...].reshape(1, H).astype(F32), 0.0).astype(BF)
    wout[...] = jnp.where(top, weight_out[...].reshape(1, H).astype(F32), 0.0).astype(BF)

    def send_all(lo, source_of, target, sem_out, sem_in):
        def body(step, carry):
            to = lax.rem(me + step, SHARDS)
            pltpu.make_async_remote_copy(
                source_of(to), target, sem_out, sem_in, (1, to), MESH
            ).start()
            return carry

        lax.fori_loop(lo, SHARDS, body, 0)

    def drain(ref, sem):
        pltpu.make_async_copy(ref, ref, sem).wait()

    @pl.when(role == 1)
    def _():
        def greet(step, carry):
            pl.semaphore_signal(barrier, inc=1, device_id=(0, step), device_id_type=MESH)

            @pl.when(step != me)
            def _():
                pl.semaphore_signal(barrier, inc=1, device_id=(1, step), device_id_type=MESH)

            return carry

        lax.fori_loop(0, SHARDS, greet, 0)

    @pl.when(role == 0)
    def _():
        pl.semaphore_signal(barrier, inc=1, device_id=(1, me), device_id_type=MESH)
        groups = lax.broadcasted_iota(jnp.int32, (SHARDS, SHARDS), 1)
        owners = lax.broadcasted_iota(jnp.int32, (SHARDS, SHARDS), 0)
        found = jnp.where(owner[...] == owners, groups, 0)
        spot = jnp.clip(jnp.sum(found, axis=1, keepdims=True), 0, SHARDS - 1)
        source_rows[...] = jnp.broadcast_to(spot, (SHARDS, E))
        fetch = pltpu.make_async_copy(source_rows, source, local.at[0])
        fetch.start()
        eye = identity()
        table_t[:, :HOT] = dot(eye, hot[...], NT).astype(BF)
        table_t[:, HOT:] = dot(eye, cold[...], NT).astype(BF)

        for slot in range(SLOTS):
            own, mult = slot_rows(ids, slot)
            lanes = slice(slot * N, (slot + 1) * N)
            for block in range(TABLE // SPAN):
                counts[block * SPAN : (block + 1) * SPAN, lanes] = count_block(own, mult, block)
            pooled_t[slot * E : (slot + 1) * E, :] = dot(table_t[...], counts[:, lanes]).astype(BF)
        first = lax.broadcasted_iota(jnp.int32, (16, N), 0) == 0
        ones = first.astype(F32).astype(BF)

        def forward(chunk, logit):
            cols = part(chunk, 256)
            pre = dot(weight[:, cols], pooled_t[...], TN) + dot(bias[:, cols], ones, TN)
            pre_t[cols, :] = pre
            hidden = (pre * sigmoid(pre)).astype(BF)
            hidden_t[cols, :] = hidden
            return logit + dot(wout[:, cols], hidden)

        logit = lax.fori_loop(0, H // 256, forward, jnp.zeros((16, N), F32))
        scores[...] = logit[0:1]
        slope = jnp.where(first, sigmoid(logit) - labels[...].reshape(1, N), 0.0).astype(BF)

        def backward(chunk, carry):
            cols = part(chunk, 256)
            pre = pre_t[cols, :]
            gate = sigmoid(pre)
            grad = (dot(wout[:, cols], slope, TN) * (gate * (1.0 + pre * (1.0 - gate)))).astype(BF)
            grad_t[cols, :] = grad
            wide[0:16, cols] = dot(ones, grad, NT)
            wide[16:32, cols] = dot(slope, hidden_t[cols, :], NT)
            return carry

        lax.fori_loop(0, H // 256, backward, 0)
        pl.semaphore_wait(barrier, SHARDS)

        def send_line(chunk, ref, sem):
            axis, first_col, width = CHUNKS[chunk]
            for step in range(4):
                index = lax.rem(coords[axis] + step, 4)
                pltpu.make_async_remote_copy(
                    line_of(ref, axis, index, pl.ds(first_col, width)),
                    rw[chunk].at[coords[axis]],
                    sem,
                    recvs.at[chunk],
                    (1, on_line(coords, axis, index)),
                    MESH,
                ).start()

        for chunk in range(3):
            _, first_col, width = CHUNKS[chunk]
            cols = pl.ds(first_col, width)

            def dense(block, carry):
                rows = dot(pooled_t[part(block, 256), :], grad_t[cols, :], NT).astype(BF)
                gw[block, :, :, :, cols] = rows.reshape(4, 4, PIECE, width)
                return carry

            lax.fori_loop(0, 4, dense, 0)
            send_line(chunk, gw, sends.at[0])

        def rows_grad(slot, carry):
            grad_rows[:, part(slot, N)] = dot(weight[part(slot, E), :], grad_t[...]).astype(BF)
            return carry

        lax.fori_loop(0, SLOTS, rows_grad, 0)
        for block in range(HOT // STEP):
            rows = dot(counts[block * STEP : (block + 1) * STEP, :], grad_rows[...], NT).astype(BF)
            gh[block * 2 : block * 2 + 2] = rows.reshape(2, 4, 4, PIECE, E)
        send_line(3, gh, sends.at[1])
        for block in range(COLD // STEP):
            rows = pl.ds(block * STEP, STEP)
            grad = dot(counts[pl.ds(HOT + block * STEP, STEP), :], grad_rows[...], NT)
            fresh = step_rows(cold[rows, :], grad)
            cold_out[rows, :] = fresh.astype(BF)
            marked = [
                jnp.where(
                    pushed[block * (STEP // BLK) + at] == 1, fresh[at * BLK : (at + 1) * BLK], unsent
                )
                for at in range(STEP // BLK)
            ]
            groups_here = pl.ds(block * (STEP // 32), STEP // 32)
            learned[groups_here] = jnp.concatenate(marked, axis=0).astype(BF).reshape(-1, 32, E)
        fetch.wait()

        def arrange(step, carry):
            outgoing[step] = learned[jnp.clip(source[step, 0], 0, SHARDS - 1)]
            return carry

        lax.fori_loop(0, SHARDS, arrange, 0)
        send_all(0, lambda to: outgoing.at[to], arrived.at[me], sends.at[2], recvs.at[16])
        for row in range(8):
            small[row : row + 1, :] = wide[0:1, row * E : (row + 1) * E]
            small[row + 8 : row + 9, :] = wide[16:17, row * E : (row + 1) * E]
        gs[...] = small[...].astype(BF)
        send_all(0, lambda to: gs, rs.at[me], sends.at[3], recvs.at[17])
        drain(gw, sends.at[0])
        drain(rs, sends.at[3])
        drain(gh, sends.at[1])
        drain(outgoing, sends.at[2])
        drain(weight_after, recvs.at[18])
        drain(hot_after, recvs.at[19])

    @pl.when(role == 1)
    def _():
        def count_slot(slot, carry):
            own, mult = slot_rows(ids, slot)
            lanes = part(slot, N)

            def build(block, carry):
                counts[part(block, SPAN), lanes] = count_block(own, mult, block)
                return carry

            return lax.fori_loop(0, TABLE // SPAN, build, carry)

        lax.fori_loop(0, SLOTS, count_slot, 0)
        pl.semaphore_wait(barrier, SHARDS)
        eye = identity()
        def add_line(chunk):
            axis = CHUNKS[chunk][0]
            drain(rw[chunk], recvs.at[chunk])

            def add(step, carry):
                at = (step // 4, lax.rem(step, 4))
                total = sum(rw[chunk][(source, *at)].astype(F32) for source in range(4))
                line[chunk][step] = total.astype(BF)
                return carry

            lax.fori_loop(0, 16, add, 0)
            own = plane_index(coords, axis)

            def send(step, carry):
                index = lax.rem(own + step, 16)
                pltpu.make_async_remote_copy(
                    line[chunk].at[index],
                    plane[chunk].at[own],
                    sends.at[chunk],
                    recvs.at[4 + chunk],
                    (1, in_plane(coords, axis, index)),
                    MESH,
                ).start()
                return carry

            lax.fori_loop(1, 16, send, 0)
            plane[chunk][own] = line[chunk][own]

        def add_plane(chunk):
            axis, first_col, width = CHUNKS[chunk]
            cols = pl.ds(first_col, width)
            drain(plane[chunk].at[pl.ds(0, 15)], recvs.at[4 + chunk])
            total = lax.fori_loop(
                0,
                16,
                lambda step, total: total + plane[chunk][step].astype(F32),
                jnp.zeros((PIECE, width), F32),
            )
            piece, whole = (piece_w, allw) if chunk < 3 else (piece_h, allh)
            if chunk == 3:
                total = step_rows(hot[part(me, PIECE), :], total)
                hot_after[...] = total.astype(BF)
            piece[:, cols] = total.astype(BF)
            whole[(*coords, slice(None), cols)] = total.astype(BF)
            own = plane_index(coords, axis)

            def send(step, carry):
                pltpu.make_async_remote_copy(
                    piece.at[:, cols],
                    whole.at[(*coords, slice(None), cols)],
                    sends.at[4 + chunk],
                    recvs.at[8 + chunk],
                    (1, in_plane(coords, axis, lax.rem(own + step, 16))),
                    MESH,
                ).start()
                return carry

            lax.fori_loop(1, 16, send, 0)

        def spread_line(chunk):
            axis, first_col, width = CHUNKS[chunk]
            cols = pl.ds(first_col, width)
            whole = allw if chunk < 3 else allh
            drain(plane[chunk].at[pl.ds(0, 15)], recvs.at[8 + chunk])
            for step in range(1, 4):
                index = lax.rem(coords[axis] + step, 4)
                pltpu.make_async_remote_copy(
                    line_of(whole, axis, coords[axis], cols),
                    line_of(whole, axis, coords[axis], cols),
                    sends.at[8 + chunk],
                    recvs.at[12 + chunk],
                    (1, on_line(coords, axis, index)),
                    MESH,
                ).start()

        for chunk in range(3):
            add_line(chunk)
        for chunk in (3,):
            add_line(chunk)
        for chunk in range(3):
            add_plane(chunk)
        for chunk in (3,):
            add_plane(chunk)
        for chunk in (3, 0, 1, 2):
            spread_line(chunk)
        drain(arrived, recvs.at[16])

        def merge(block, carry):
            rows = part(block, SPAN)
            came = arrived[part(block, 8)].reshape(SPAN, E)
            fresh = jnp.where(came < unsent * 0.5, came, cold[rows, :])
            cold_out[rows, :] = fresh
            table_t[:, pl.ds(pl.multiple_of(HOT + block * SPAN, SPAN), SPAN)] = dot(eye, fresh, NT).astype(BF)
            return carry

        lax.fori_loop(0, COLD // SPAN, merge, 0)

        def pool_cold(slot, carry):
            pool_acc[part(slot, E), :] = dot(table_t[:, HOT:], counts[HOT:, part(slot, N)])
            return carry

        lax.fori_loop(0, SLOTS, pool_cold, 0)
        drain(rw[3].at[pl.ds(0, 3)], recvs.at[15])
        table_t[:, :HOT] = dot(eye, allh[...].reshape(HOT, E), NT).astype(BF)

        def pool_hot(slot, carry):
            rows = part(slot, E)
            pooled_t[rows, :] = (
                pool_acc[rows, :] + dot(table_t[:, :HOT], counts[:HOT, part(slot, N)])
            ).astype(BF)
            return carry

        lax.fori_loop(0, SLOTS, pool_hot, 0)
        ones = (lax.broadcasted_iota(jnp.int32, (16, N), 0) == 0).astype(F32).astype(BF)

        def before(chunk, carry):
            cols = part(chunk, 256)
            pre_t[cols, :] = dot(weight[:, cols], pooled_t[...], TN)
            return carry

        lax.fori_loop(0, H // 256, before, 0)
        drain(rs, recvs.at[17])
        sums = lax.fori_loop(
            0,
            SHARDS,
            lambda step, total: total + rs[step].astype(F32),
            jnp.zeros((16, E), F32),
        )
        bias_sum, out_sum = sums[:8], sums[8:]
        bias_scale = 0.5 / jnp.sqrt(jnp.mean(bias_sum * bias_sum, keepdims=True) + epsilon)
        out_scale = (1.0 / math.sqrt(H)) / jnp.sqrt(jnp.mean(out_sum * out_sum, keepdims=True) + epsilon)
        small[0:8, :] = bias_sum * bias_scale
        small[8:16, :] = out_sum * out_scale
        wide[...] = jnp.zeros(wide.shape, F32)
        for row in range(8):
            wide[0:1, row * E : (row + 1) * E] = small[row : row + 1, :]
            wide[16:17, row * E : (row + 1) * E] = small[row + 8 : row + 9, :]
        bias_next = (bias[...].astype(F32) - wide[0:16, :]).astype(BF)
        out_next = (wout[...].astype(F32) - wide[16:32, :]).astype(BF)
        small16 = bias_next, out_next
        wide[0:16, :] = small16[0].astype(F32)
        wide[16:32, :] = small16[1].astype(F32)

        for chunk in range(3):
            drain(rw[chunk].at[pl.ds(0, 3)], recvs.at[12 + chunk])

        for chunk in range(4):
            drain(plane[chunk].at[pl.ds(0, 15)], sends.at[chunk])
            drain(plane[chunk].at[pl.ds(0, 15)], sends.at[4 + chunk])
            drain(rw[chunk].at[pl.ds(0, 3)], sends.at[8 + chunk])

        def squares(step, total):
            value = allw[step // 16, lax.rem(step // 4, 4), lax.rem(step, 4)].astype(F32)
            return total + value * value

        total = lax.fori_loop(0, SHARDS, squares, jnp.zeros((PIECE, H), F32))
        scale = (1.0 / math.sqrt(H)) / jnp.sqrt(jnp.sum(total, keepdims=True) / (H * H) + epsilon)

        weight_after[...] = (
            weight[part(me, PIECE), :].astype(F32) - allw[coords].astype(F32) * scale
        ).astype(BF)
        piece_w[...] = weight_after[...]
        final_w = pltpu.make_async_remote_copy(
            piece_w, weight_after, sends.at[12], recvs.at[18], (0, me), MESH
        )
        final_h = pltpu.make_async_remote_copy(
            piece_h, hot_after, sends.at[13], recvs.at[19], (0, me), MESH
        )
        final_w.start()
        final_h.start()

        def score(chunk, logit):
            cols = part(chunk, 256)
            grad = allw[:, :, :, :, cols].reshape(H, 256)
            pre = pre_t[cols, :] - dot(grad, pooled_t[...], TN) * scale
            pre = pre + dot(wide[0:16, cols].astype(BF), ones, TN)
            hidden = (pre * sigmoid(pre)).astype(BF)
            return logit + dot(wide[16:32, cols].astype(BF), hidden)

        scores[...] = lax.fori_loop(0, H // 256, score, jnp.zeros((16, N), F32))[0:1]
        final_w.wait_send()
        final_h.wait_send()


def run_round(ids, labels, hot, cold, weight, bias, wout, owner, pushed):
    vmem = pl.BlockSpec(memory_space=pltpu.VMEM)
    smem = pl.BlockSpec(memory_space=pltpu.SMEM)
    return pl.pallas_call(
        round_kernel,
        out_shape=(
            jax.ShapeDtypeStruct((1, N), F32),
            jax.ShapeDtypeStruct((COLD, E), BF),
            jax.ShapeDtypeStruct((PIECE, E), BF),
            jax.ShapeDtypeStruct((PIECE, H), BF),
        ),
        in_specs=[vmem] * 8 + [smem],
        out_specs=(vmem,) * 4,
        scratch_shapes=[
            pltpu.VMEM((TABLE, SLOTS * N), BF),
            pltpu.VMEM((E, TABLE), BF),
            pltpu.VMEM((H, N), BF),
            pltpu.VMEM((H, N), F32),
            pltpu.VMEM((H, N), BF),
            pltpu.VMEM((H, N), BF),
            pltpu.VMEM((E, SLOTS * N), BF),
            pltpu.VMEM((H, N), F32),
            pltpu.VMEM((4, 4, 4, PIECE, H), BF),
            *[pltpu.VMEM((4, 4, 4, PIECE, width), BF) for _, _, width in CHUNKS],
            *[pltpu.VMEM((16, PIECE, width), BF) for _, _, width in CHUNKS],
            *[pltpu.VMEM((16, PIECE, width), BF) for _, _, width in CHUNKS],
            pltpu.VMEM((4, 4, 4, PIECE, H), BF),
            pltpu.VMEM((4, 4, 4, PIECE, E), BF),
            pltpu.VMEM((16, E), BF),
            pltpu.VMEM((SHARDS, 16, E), BF),
            pltpu.VMEM((4, 4, 4, PIECE, E), BF),
            pltpu.VMEM((PIECE, H), BF),
            pltpu.VMEM((PIECE, E), BF),
            pltpu.VMEM((SHARDS, 32, E), BF),
            pltpu.VMEM((SHARDS, 32, E), BF),
            pltpu.VMEM((SHARDS, 32, E), BF),
            pltpu.VMEM((16, E), F32),
            pltpu.VMEM((32, H), F32),
            pltpu.VMEM((16, H), BF),
            pltpu.VMEM((16, H), BF),
            pltpu.VMEM((SHARDS, E), jnp.int32),
            pltpu.SMEM((SHARDS, E), jnp.int32),
            pltpu.SemaphoreType.DMA((14,)),
            pltpu.SemaphoreType.DMA((20,)),
            pltpu.SemaphoreType.DMA((1,)),
        ],
        compiler_params=pltpu.CompilerParams(
            collective_id=0, has_side_effects=True, vmem_limit_bytes=58 << 20
        ),
        name="round",
    )(ids, labels, hot, cold, weight, bias, wout, owner, pushed)


def hand_over_kernel(*refs):
    count = len(refs) // 2
    copies = [
        pltpu.make_async_copy(refs[at], refs[count + at], refs[-1].at[at]) for at in range(count)
    ]
    for copy in copies:
        copy.start()
    for copy in copies:
        copy.wait()


def hand_over(arrays):
    return pl.pallas_call(
        hand_over_kernel,
        out_shape=tuple(jax.ShapeDtypeStruct(array.shape, array.dtype) for array in arrays),
        in_specs=[pl.BlockSpec(memory_space=pl.ANY)] * len(arrays),
        out_specs=(pl.BlockSpec(memory_space=pltpu.VMEM),) * len(arrays),
        scratch_shapes=[pltpu.SemaphoreType.DMA((len(arrays),))],
        name="hand_over",
    )(*arrays)


def on_device(
    feature_ids, labels, cold_rows, hot_rows, block_owner, pushed, weight_in, bias_in, weight_out
):
    scores, cold_out, hot_after, weight_after = hand_over(
        run_round(
            feature_ids[0],
            labels,
            hot_rows,
            cold_rows[0],
            weight_in,
            bias_in,
            weight_out,
            block_owner,
            pushed,
        )
    )
    return (scores, cold_out[None], hot_after, weight_after)


def solution(mesh):
    in_specs = (
        P("role", None, None, "shard"),
        P("shard"),
        P("role", "shard", None),
        P(),
        P("shard", None),
        P("shard"),
        P(),
        P(),
        P(),
    )
    out_specs = (P("role", "shard"), P("role", "shard", None), P("shard", None), P("shard", None))
    return jax.shard_map(
        on_device, mesh=mesh, in_specs=in_specs, out_specs=out_specs, check_vma=False
    )
```

```python
import math

import jax
import jax.numpy as jnp
from jax import lax
from jax.experimental import pallas as pl
from jax.experimental.pallas import tpu as pltpu
from jax.sharding import PartitionSpec as P

row_rate = 0.25
epsilon = 1e-06
unsent = 1e30
BF = jnp.bfloat16
F32 = jnp.float32
MESH = pl.DeviceIdType.MESH
NN = (((1,), (0,)), ((), ()))
NT = (((1,), (1,)), ((), ()))
TN = (((0,), (0,)), ((), ()))

SHARDS = 64
SLOTS = 8
BAGS = 4
N = 512
E = 128
H = 1024
HOT = 1024
COLD = 2048
TABLE = HOT + COLD
PIECE = H // SHARDS
BLK = 8
SPAN = 256
STEP = 512
CHUNKS = ((0, 0, 384), (1, 384, 384), (2, 768, 256), (1, 0, 128))


def dot(lhs, rhs, dims=NN):
    return lax.dot_general(lhs, rhs, dims, preferred_element_type=F32)


def sigmoid(value):
    return 0.5 * jnp.tanh(0.5 * value) + 0.5


def step_rows(old_rows, grad_rows):
    scale_rows = row_rate * lax.rsqrt(jnp.mean(grad_rows * grad_rows, axis=-1, keepdims=True) + epsilon)
    return old_rows.astype(F32) - grad_rows * scale_rows


def part(index, size):
    return pl.ds(pl.multiple_of(index * size, size), size)


def identity():
    rows = lax.broadcasted_iota(jnp.int32, (E, E), 0)
    return (rows == lax.broadcasted_iota(jnp.int32, (E, E), 1)).astype(F32).astype(BF)


def first_row(value):
    return lax.broadcasted_iota(jnp.int32, (16, N), 0) == 0


def slot_rows(ids, slot):
    own = [ids[slot, bag][None, :] for bag in range(BAGS)]
    mult = [sum((one == other).astype(F32) for other in own).astype(BF) for one in own]
    return own, mult


def count_block(own, mult, block):
    spots = lax.broadcasted_iota(jnp.int32, (SPAN, N), 0).astype(F32).astype(BF)
    acc = jnp.zeros((SPAN, N), BF)
    for bag in range(BAGS):
        at = jnp.clip(own[bag] - block * SPAN, -1, SPAN).astype(F32).astype(BF)
        acc = jnp.where(spots == at, mult[bag], acc)
    return acc


def line_of(ref, axis, index, cols):
    at = [slice(None)] * 3
    at[axis] = index
    return ref.at[(*at, slice(None), cols)]


def shard_of(coords):
    return coords[0] * 16 + coords[1] * 4 + coords[2]


def on_line(coords, axis, index):
    return shard_of([index if other == axis else coords[other] for other in range(3)])


def in_plane(coords, axis, index):
    spots = iter((index // 4, lax.rem(index, 4)))
    return shard_of([coords[axis] if other == axis else next(spots) for other in range(3)])


def plane_index(coords, axis):
    first, second = [coords[other] for other in range(3) if other != axis]
    return first * 4 + second


def round_kernel(
    ids, labels, hot, cold, weight, bias_in, weight_out, owner, pushed,
    scores, cold_out, hot_after, weight_after,
    counts, table_t, pooled_t, pre_t, hidden_t, grad_t, grad_rows, pool_acc,
    gw, rw0, rw1, rw2, rw3, line0, line1, line2, line3, plane0, plane1, plane2, plane3, allw, gh, gs, rs, allh, piece_w, piece_h, learned, outgoing, arrived, small, wide,
    bias, wout, source_rows, source, sends, recvs, local,
):
    role = lax.axis_index("role")
    me = lax.axis_index("shard")
    coords = (me // 16, lax.rem(me // 4, 4), lax.rem(me, 4))
    rw, line = (rw0, rw1, rw2, rw3), (line0, line1, line2, line3)
    plane = (plane0, plane1, plane2, plane3)
    barrier = pltpu.get_barrier_semaphore()
    top = lax.broadcasted_iota(jnp.int32, (16, H), 0) == 0
    bias[...] = jnp.where(top, bias_in[...].reshape(1, H).astype(F32), 0.0).astype(BF)
    wout[...] = jnp.where(top, weight_out[...].reshape(1, H).astype(F32), 0.0).astype(BF)

    def send_all(lo, source_of, target, sem_out, sem_in):
        def body(step, carry):
            to = lax.rem(me + step, SHARDS)
            pltpu.make_async_remote_copy(
                source_of(to), target, sem_out, sem_in, (1, to), MESH
            ).start()
            return carry

        lax.fori_loop(lo, SHARDS, body, 0)

    def drain(ref, sem):
        pltpu.make_async_copy(ref, ref, sem).wait()

    @pl.when(role == 1)
    def _():
        def greet(step, carry):
            pl.semaphore_signal(barrier, inc=1, device_id=(0, step), device_id_type=MESH)

            @pl.when(step != me)
            def _():
                pl.semaphore_signal(barrier, inc=1, device_id=(1, step), device_id_type=MESH)

            return carry

        lax.fori_loop(0, SHARDS, greet, 0)

    @pl.when(role == 0)
    def _():
        pl.semaphore_signal(barrier, inc=1, device_id=(1, me), device_id_type=MESH)
        groups = lax.broadcasted_iota(jnp.int32, (SHARDS, SHARDS), 1)
        owners = lax.broadcasted_iota(jnp.int32, (SHARDS, SHARDS), 0)
        found = jnp.where(owner[...] == owners, groups, 0)
        spot = jnp.clip(jnp.sum(found, axis=1, keepdims=True), 0, SHARDS - 1)
        source_rows[...] = jnp.broadcast_to(spot, (SHARDS, E))
        fetch = pltpu.make_async_copy(source_rows, source, local.at[0])
        fetch.start()
        eye = identity()
        table_t[:, :HOT] = dot(eye, hot[...], NT).astype(BF)
        table_t[:, HOT:] = dot(eye, cold[...], NT).astype(BF)

        for slot in range(SLOTS):
            own, mult = slot_rows(ids, slot)
            lanes = slice(slot * N, (slot + 1) * N)
            for block in range(TABLE // SPAN):
                counts[block * SPAN : (block + 1) * SPAN, lanes] = count_block(own, mult, block)
            pooled_t[slot * E : (slot + 1) * E, :] = dot(table_t[...], counts[:, lanes]).astype(BF)
        first = lax.broadcasted_iota(jnp.int32, (16, N), 0) == 0
        ones = first.astype(F32).astype(BF)

        def forward(chunk, logit):
            cols = part(chunk, 256)
            pre = dot(weight[:, cols], pooled_t[...], TN) + dot(bias[:, cols], ones, TN)
            pre_t[cols, :] = pre
            hidden = (pre * sigmoid(pre)).astype(BF)
            hidden_t[cols, :] = hidden
            return logit + dot(wout[:, cols], hidden)

        logit = lax.fori_loop(0, H // 256, forward, jnp.zeros((16, N), F32), unroll=True)
        scores[...] = logit[0:1]
        slope = jnp.where(first, sigmoid(logit) - labels[...].reshape(1, N), 0.0).astype(BF)

        def backward(chunk, carry):
            cols = part(chunk, 256)
            pre = pre_t[cols, :]
            gate = sigmoid(pre)
            grad = (dot(wout[:, cols], slope, TN) * (gate * (1.0 + pre * (1.0 - gate)))).astype(BF)
            grad_t[cols, :] = grad
            wide[0:16, cols] = dot(ones, grad, NT)
            wide[16:32, cols] = dot(slope, hidden_t[cols, :], NT)
            return carry

        lax.fori_loop(0, H // 256, backward, 0, unroll=True)
        pl.semaphore_wait(barrier, SHARDS)

        def send_line(chunk, ref, sem):
            axis, first_col, width = CHUNKS[chunk]
            for step in range(4):
                index = lax.rem(coords[axis] + step, 4)
                pltpu.make_async_remote_copy(
                    line_of(ref, axis, index, pl.ds(first_col, width)),
                    rw[chunk].at[coords[axis]],
                    sem,
                    recvs.at[chunk],
                    (1, on_line(coords, axis, index)),
                    MESH,
                ).start()

        for chunk in range(3):
            _, first_col, width = CHUNKS[chunk]
            cols = pl.ds(first_col, width)

            def dense(block, carry):
                rows = dot(pooled_t[part(block, 256), :], grad_t[cols, :], NT).astype(BF)
                gw[block, :, :, :, cols] = rows.reshape(4, 4, PIECE, width)
                return carry

            lax.fori_loop(0, 4, dense, 0, unroll=True)
            send_line(chunk, gw, sends.at[0])

        def rows_grad(slot, carry):
            grad_rows[:, part(slot, N)] = dot(weight[part(slot, E), :], grad_t[...]).astype(BF)
            return carry

        lax.fori_loop(0, SLOTS, rows_grad, 0)
        for block in range(HOT // STEP):
            rows = dot(counts[block * STEP : (block + 1) * STEP, :], grad_rows[...], NT).astype(BF)
            gh[block * 2 : block * 2 + 2] = rows.reshape(2, 4, 4, PIECE, E)
        send_line(3, gh, sends.at[1])
        for block in range(COLD // STEP):
            rows = pl.ds(block * STEP, STEP)
            grad = dot(counts[pl.ds(HOT + block * STEP, STEP), :], grad_rows[...], NT)
            fresh = step_rows(cold[rows, :], grad)
            cold_out[rows, :] = fresh.astype(BF)
            marked = [
                jnp.where(
                    pushed[block * (STEP // BLK) + at] == 1, fresh[at * BLK : (at + 1) * BLK], unsent
                )
                for at in range(STEP // BLK)
            ]
            groups_here = pl.ds(block * (STEP // 32), STEP // 32)
            learned[groups_here] = jnp.concatenate(marked, axis=0).astype(BF).reshape(-1, 32, E)
        fetch.wait()

        def arrange(step, carry):
            outgoing[step] = learned[jnp.clip(source[step, 0], 0, SHARDS - 1)]
            return carry

        lax.fori_loop(0, SHARDS, arrange, 0)
        send_all(0, lambda to: outgoing.at[to], arrived.at[me], sends.at[2], recvs.at[16])
        for row in range(8):
            small[row : row + 1, :] = wide[0:1, row * E : (row + 1) * E]
            small[row + 8 : row + 9, :] = wide[16:17, row * E : (row + 1) * E]
        gs[...] = small[...].astype(BF)
        send_all(0, lambda to: gs, rs.at[me], sends.at[3], recvs.at[17])
        drain(gw, sends.at[0])
        drain(rs, sends.at[3])
        drain(gh, sends.at[1])
        drain(outgoing, sends.at[2])
        drain(weight_after, recvs.at[18])
        drain(hot_after, recvs.at[19])

    @pl.when(role == 1)
    def _():
        def count_slot(slot, carry):
            own, mult = slot_rows(ids, slot)
            lanes = part(slot, N)

            def build(block, carry):
                counts[part(block, SPAN), lanes] = count_block(own, mult, block)
                return carry

            return lax.fori_loop(0, TABLE // SPAN, build, carry)

        lax.fori_loop(0, SLOTS, count_slot, 0)
        pl.semaphore_wait(barrier, SHARDS)
        eye = identity()
        def add_line(chunk):
            axis = CHUNKS[chunk][0]
            drain(rw[chunk], recvs.at[chunk])

            def add(step, carry):
                at = (step // 4, lax.rem(step, 4))
                total = sum(rw[chunk][(source, *at)].astype(F32) for source in range(4))
                line[chunk][step] = total.astype(BF)
                return carry

            lax.fori_loop(0, 16, add, 0, unroll=4)
            own = plane_index(coords, axis)

            def send(step, carry):
                index = lax.rem(own + step, 16)
                pltpu.make_async_remote_copy(
                    line[chunk].at[index],
                    plane[chunk].at[own],
                    sends.at[chunk],
                    recvs.at[4 + chunk],
                    (1, in_plane(coords, axis, index)),
                    MESH,
                ).start()
                return carry

            lax.fori_loop(1, 16, send, 0)
            plane[chunk][own] = line[chunk][own]

        def add_plane(chunk):
            axis, first_col, width = CHUNKS[chunk]
            cols = pl.ds(first_col, width)
            drain(plane[chunk].at[pl.ds(0, 15)], recvs.at[4 + chunk])
            total = lax.fori_loop(
                0,
                16,
                lambda step, total: total + plane[chunk][step].astype(F32),
                jnp.zeros((PIECE, width), F32),
            )
            piece, whole = (piece_w, allw) if chunk < 3 else (piece_h, allh)
            if chunk == 3:
                total = step_rows(hot[part(me, PIECE), :], total)
                hot_after[...] = total.astype(BF)
            piece[:, cols] = total.astype(BF)
            whole[(*coords, slice(None), cols)] = total.astype(BF)
            own = plane_index(coords, axis)

            def send(step, carry):
                pltpu.make_async_remote_copy(
                    piece.at[:, cols],
                    whole.at[(*coords, slice(None), cols)],
                    sends.at[4 + chunk],
                    recvs.at[8 + chunk],
                    (1, in_plane(coords, axis, lax.rem(own + step, 16))),
                    MESH,
                ).start()
                return carry

            lax.fori_loop(1, 16, send, 0)

        def spread_line(chunk):
            axis, first_col, width = CHUNKS[chunk]
            cols = pl.ds(first_col, width)
            whole = allw if chunk < 3 else allh
            drain(plane[chunk].at[pl.ds(0, 15)], recvs.at[8 + chunk])
            for step in range(1, 4):
                index = lax.rem(coords[axis] + step, 4)
                pltpu.make_async_remote_copy(
                    line_of(whole, axis, coords[axis], cols),
                    line_of(whole, axis, coords[axis], cols),
                    sends.at[8 + chunk],
                    recvs.at[12 + chunk],
                    (1, on_line(coords, axis, index)),
                    MESH,
                ).start()

        for chunk in range(3):
            add_line(chunk)
        for chunk in (3,):
            add_line(chunk)
        for chunk in range(3):
            add_plane(chunk)
        for chunk in (3,):
            add_plane(chunk)
        for chunk in (3, 0, 1, 2):
            spread_line(chunk)
        drain(arrived, recvs.at[16])

        def merge(block, carry):
            rows = part(block, SPAN)
            came = arrived[part(block, 8)].reshape(SPAN, E)
            fresh = jnp.where(came < unsent * 0.5, came, cold[rows, :])
            cold_out[rows, :] = fresh
            table_t[:, pl.ds(pl.multiple_of(HOT + block * SPAN, SPAN), SPAN)] = dot(eye, fresh, NT).astype(BF)
            return carry

        lax.fori_loop(0, COLD // SPAN, merge, 0, unroll=True)

        def pool_cold(slot, carry):
            pool_acc[part(slot, E), :] = dot(table_t[:, HOT:], counts[HOT:, part(slot, N)])
            return carry

        lax.fori_loop(0, SLOTS, pool_cold, 0)
        drain(rw[3].at[pl.ds(0, 3)], recvs.at[15])
        table_t[:, :HOT] = dot(eye, allh[...].reshape(HOT, E), NT).astype(BF)

        def pool_hot(slot, carry):
            rows = part(slot, E)
            pooled_t[rows, :] = (
                pool_acc[rows, :] + dot(table_t[:, :HOT], counts[:HOT, part(slot, N)])
            ).astype(BF)
            return carry

        lax.fori_loop(0, SLOTS, pool_hot, 0)
        ones = (lax.broadcasted_iota(jnp.int32, (16, N), 0) == 0).astype(F32).astype(BF)

        def before(chunk, carry):
            cols = part(chunk, 256)
            pre_t[cols, :] = dot(weight[:, cols], pooled_t[...], TN)
            return carry

        lax.fori_loop(0, H // 256, before, 0, unroll=True)
        drain(rs, recvs.at[17])
        sums = lax.fori_loop(
            0,
            SHARDS,
            lambda step, total: total + rs[step].astype(F32),
            jnp.zeros((16, E), F32),
        )
        bias_sum, out_sum = sums[:8], sums[8:]
        bias_scale = 0.5 / jnp.sqrt(jnp.mean(bias_sum * bias_sum, keepdims=True) + epsilon)
        out_scale = (1.0 / math.sqrt(H)) / jnp.sqrt(jnp.mean(out_sum * out_sum, keepdims=True) + epsilon)
        small[0:8, :] = bias_sum * bias_scale
        small[8:16, :] = out_sum * out_scale
        wide[...] = jnp.zeros(wide.shape, F32)
        for row in range(8):
            wide[0:1, row * E : (row + 1) * E] = small[row : row + 1, :]
            wide[16:17, row * E : (row + 1) * E] = small[row + 8 : row + 9, :]
        bias_next = (bias[...].astype(F32) - wide[0:16, :]).astype(BF)
        out_next = (wout[...].astype(F32) - wide[16:32, :]).astype(BF)
        small16 = bias_next, out_next
        wide[0:16, :] = small16[0].astype(F32)
        wide[16:32, :] = small16[1].astype(F32)

        for chunk in range(3):
            drain(rw[chunk].at[pl.ds(0, 3)], recvs.at[12 + chunk])

        for chunk in range(4):
            drain(plane[chunk].at[pl.ds(0, 15)], sends.at[chunk])
            drain(plane[chunk].at[pl.ds(0, 15)], sends.at[4 + chunk])
            drain(rw[chunk].at[pl.ds(0, 3)], sends.at[8 + chunk])

        def squares(step, total):
            value = allw[step // 16, lax.rem(step // 4, 4), lax.rem(step, 4)].astype(F32)
            return total + value * value

        total = lax.fori_loop(0, SHARDS, squares, jnp.zeros((PIECE, H), F32), unroll=8)
        scale = (1.0 / math.sqrt(H)) / jnp.sqrt(jnp.sum(total, keepdims=True) / (H * H) + epsilon)

        weight_after[...] = (
            weight[part(me, PIECE), :].astype(F32) - allw[coords].astype(F32) * scale
        ).astype(BF)
        piece_w[...] = weight_after[...]
        final_w = pltpu.make_async_remote_copy(
            piece_w, weight_after, sends.at[12], recvs.at[18], (0, me), MESH
        )
        final_h = pltpu.make_async_remote_copy(
            piece_h, hot_after, sends.at[13], recvs.at[19], (0, me), MESH
        )
        final_w.start()
        final_h.start()

        def score(chunk, logit):
            cols = part(chunk, 256)
            grad = allw[:, :, :, :, cols].reshape(H, 256)
            pre = pre_t[cols, :] - dot(grad, pooled_t[...], TN) * scale
            pre = pre + dot(wide[0:16, cols].astype(BF), ones, TN)
            hidden = (pre * sigmoid(pre)).astype(BF)
            return logit + dot(wide[16:32, cols].astype(BF), hidden)

        scores[...] = lax.fori_loop(0, H // 256, score, jnp.zeros((16, N), F32), unroll=True)[0:1]
        final_w.wait_send()
        final_h.wait_send()


def run_round(ids, labels, hot, cold, weight, bias, wout, owner, pushed):
    vmem = pl.BlockSpec(memory_space=pltpu.VMEM)
    smem = pl.BlockSpec(memory_space=pltpu.SMEM)
    return pl.pallas_call(
        round_kernel,
        out_shape=(
            jax.ShapeDtypeStruct((1, N), F32),
            jax.ShapeDtypeStruct((COLD, E), BF),
            jax.ShapeDtypeStruct((PIECE, E), BF),
            jax.ShapeDtypeStruct((PIECE, H), BF),
        ),
        in_specs=[vmem] * 8 + [smem],
        out_specs=(vmem,) * 4,
        scratch_shapes=[
            pltpu.VMEM((TABLE, SLOTS * N), BF),
            pltpu.VMEM((E, TABLE), BF),
            pltpu.VMEM((H, N), BF),
            pltpu.VMEM((H, N), F32),
            pltpu.VMEM((H, N), BF),
            pltpu.VMEM((H, N), BF),
            pltpu.VMEM((E, SLOTS * N), BF),
            pltpu.VMEM((H, N), F32),
            pltpu.VMEM((4, 4, 4, PIECE, H), BF),
            *[pltpu.VMEM((4, 4, 4, PIECE, width), BF) for _, _, width in CHUNKS],
            *[pltpu.VMEM((16, PIECE, width), BF) for _, _, width in CHUNKS],
            *[pltpu.VMEM((16, PIECE, width), BF) for _, _, width in CHUNKS],
            pltpu.VMEM((4, 4, 4, PIECE, H), BF),
            pltpu.VMEM((4, 4, 4, PIECE, E), BF),
            pltpu.VMEM((16, E), BF),
            pltpu.VMEM((SHARDS, 16, E), BF),
            pltpu.VMEM((4, 4, 4, PIECE, E), BF),
            pltpu.VMEM((PIECE, H), BF),
            pltpu.VMEM((PIECE, E), BF),
            pltpu.VMEM((SHARDS, 32, E), BF),
            pltpu.VMEM((SHARDS, 32, E), BF),
            pltpu.VMEM((SHARDS, 32, E), BF),
            pltpu.VMEM((16, E), F32),
            pltpu.VMEM((32, H), F32),
            pltpu.VMEM((16, H), BF),
            pltpu.VMEM((16, H), BF),
            pltpu.VMEM((SHARDS, E), jnp.int32),
            pltpu.SMEM((SHARDS, E), jnp.int32),
            pltpu.SemaphoreType.DMA((14,)),
            pltpu.SemaphoreType.DMA((20,)),
            pltpu.SemaphoreType.DMA((1,)),
        ],
        compiler_params=pltpu.CompilerParams(
            collective_id=0, has_side_effects=True, vmem_limit_bytes=58 << 20
        ),
        name="round",
    )(ids, labels, hot, cold, weight, bias, wout, owner, pushed)


def hand_over_kernel(*refs):
    count = len(refs) // 2
    copies = [
        pltpu.make_async_copy(refs[at], refs[count + at], refs[-1].at[at]) for at in range(count)
    ]
    for copy in copies:
        copy.start()
    for copy in copies:
        copy.wait()


def hand_over(arrays):
    return pl.pallas_call(
        hand_over_kernel,
        out_shape=tuple(jax.ShapeDtypeStruct(array.shape, array.dtype) for array in arrays),
        in_specs=[pl.BlockSpec(memory_space=pl.ANY)] * len(arrays),
        out_specs=(pl.BlockSpec(memory_space=pltpu.VMEM),) * len(arrays),
        scratch_shapes=[pltpu.SemaphoreType.DMA((len(arrays),))],
        name="hand_over",
    )(*arrays)


def on_device(
    feature_ids, labels, cold_rows, hot_rows, block_owner, pushed, weight_in, bias_in, weight_out
):
    scores, cold_out, hot_after, weight_after = hand_over(
        run_round(
            feature_ids[0],
            labels,
            hot_rows,
            cold_rows[0],
            weight_in,
            bias_in,
            weight_out,
            block_owner,
            pushed,
        )
    )
    return (scores, cold_out[None], hot_after, weight_after)


def solution(mesh):
    in_specs = (
        P("role", None, None, "shard"),
        P("shard"),
        P("role", "shard", None),
        P(),
        P("shard", None),
        P("shard"),
        P(),
        P(),
        P(),
    )
    out_specs = (P("role", "shard"), P("role", "shard", None), P("shard", None), P("shard", None))
    return jax.shard_map(
        on_device, mesh=mesh, in_specs=in_specs, out_specs=out_specs, check_vma=False
    )
```
